32 devices in a mesh: member: 2 (over y), lat: 8 (over z, x), lev: 2 (over core).
Axes of the slice: x: 2, y: 2, z: 4, core: 2. Of those that a mesh axis runs over, the one named last changes fastest.
Arguments:
- grid: bfloat16 [4, 96, 768, 1536], P('member', 'lev', 'lat'), parts along dimension 0, may hold values from -6 to 6
- w_in: bfloat16 [384, 192], replicated, may hold values from -0.4375 to 0.4375
- b_in: float32 [384], replicated, may hold values from -3 to 3
- w_out: bfloat16 [192, 384], replicated, may hold values from -0.3125 to 0.3125
- lat_weight: float32 [768], P('lat'), may hold values from 0.5 to 2
- legendre: bfloat16 [256, 513, 768], P(('lat', 'lev')), may hold values from -0.21875 to 0.21875
- order_table: int32 [256], replicated, may hold values from 0 to 255, each once
- modes: float32 [96, 96], replicated, may hold values from -0.625 to 0.625
- depths: float32 [96], replicated, may hold values from 0.05 to 2
Outputs:
- new_grid: bfloat16 [4, 96, 768, 1536], P('member', 'lev', 'lat'), parts along dimension 0
The draws below stay inside these ranges and needn't reach their ends.
There are 2 independent parts, one for each index of `member`. The reference program is written for one: setup_inputs(seed, part) draws one part's arguments, and reference() takes and returns one part's arrays. A program takes and returns all parts, laid end to end along the dimension named above; an argument that names none is the same for every part. Nothing has to cross between parts.
Inputs may be any that keep to these rules, and one draw needn't show every extreme that they name: `order_table`: each of 0 to 255 appears once.
All inputs are finite; a program needn't handle non-finite values.
Results may differ from the reference program's by a relative error of at most 0.0075.
Values may be sent and summed in bfloat16 or wider, within the bound.
No kernel may reach another device: no remote copies, remote signals or barrier semaphores. Data moves between devices by JAX's collectives and lax.ppermute only.
A program may use at most 320 MiB of HBM per device.

```python
import math
import jax
import jax.numpy as jnp
from jax import lax

FIELDS = 2
LEVELS = 96
NLAT = 768
NLON = 1536
ORDERS = 512
HID = 384
PAIRS = 256
DEGS = 513


def steps_of(stream_key, extent, shards, smallest, high):
    loudness, own = 1.0, jax.random.fold_in(stream_key, 6)
    for dim, parts in shards:
        steps = jnp.exp(jax.random.uniform(jax.random.fold_in(own, dim), (parts,), jnp.float32, smallest / len(shards), high / len(shards)))
        loudness = loudness * jnp.repeat(steps, extent[dim] // parts).reshape([-1 if axis == dim else 1 for axis in range(len(extent))])
    return loudness


def noise(key, extent, deviation, most, cuts=(), kind=jnp.bfloat16):
    gain = steps_of(key, extent, cuts, -0.22, 0.18) if cuts else 1.0
    values = jax.random.normal(key, extent, jnp.float32) * deviation * gain
    return jnp.minimum(jnp.maximum(values, -most), most).astype(kind)


def setup_inputs(seed: int = 0, part: int = 0) -> dict:
    seeds = jax.random.split(jax.random.key(seed), 10)
    part_keys = jax.random.split(jax.random.fold_in(seeds[9], part), 10)
    return {
        "grid": noise(part_keys[0], (FIELDS, LEVELS, NLAT, NLON), 1.0, 6.0, ((1, 2), (2, 8))),
        "w_in": noise(seeds[1], (HID, FIELDS * LEVELS), (FIELDS * LEVELS) ** -0.5, 0.4375),
        "b_in": noise(seeds[2], (HID,), 0.5, 3.0, (), jnp.float32),
        "w_out": noise(seeds[3], (FIELDS * LEVELS, HID), HID ** -0.5, 0.3125),
        "lat_weight": jnp.clip(jnp.exp(math.log(2.0) - 1.3862944 * jax.random.uniform(seeds[4], (NLAT,), jnp.float32) ** steps_of(seeds[4], (NLAT,), ((0, 8),), -0.2, 0.2)), 0.5, 2.0),
        "legendre": noise(seeds[5], (PAIRS, DEGS, NLAT), NLAT ** -0.5, 0.21875, ((0, 16),)),
        "order_table": jax.random.permutation(seeds[6], PAIRS).astype(jnp.int32),
        "modes": noise(seeds[7], (LEVELS, LEVELS), LEVELS ** -0.5, 0.625, (), jnp.float32),
        "depths": jnp.clip(jnp.exp(jax.random.uniform(seeds[8], (LEVELS,), jnp.float32, math.log(0.05), math.log(2.0))), 0.05, 2.0),
    }


time_step = 1.0

def fourier_table(slot_orders, lon_count, order_count):
    upper = order_count - 1 - slot_orders
    orders = jnp.stack([slot_orders, slot_orders, upper, upper], axis=-1).reshape(-1).astype(jnp.int32)
    parity = jnp.tile(jnp.arange(2, dtype=jnp.int32), 2 * slot_orders.shape[0])
    longitude = jnp.arange(lon_count, dtype=jnp.int32)
    phases = longitude[:, None] * orders[None, :] % lon_count
    angles = phases.astype(jnp.float32) * (2.0 * math.pi / lon_count)
    return jnp.where(parity[None, :] == 0, jnp.cos(angles), -jnp.sin(angles)).astype(jnp.bfloat16)

def column_physics(columns, w_in, b_in, w_out):
    hidden = jnp.dot(w_in, columns, preferred_element_type=jnp.float32) + b_in[:, None]
    hidden = jax.nn.silu(hidden).astype(jnp.bfloat16)
    change = jnp.dot(w_out, hidden, preferred_element_type=jnp.float32)
    return (columns.astype(jnp.float32) + change).astype(jnp.bfloat16)

def implicit_update(spectral, coeff, modes, depths):
    highest = lax.Precision.HIGHEST
    modal = jnp.einsum('...l,lj->...j', spectral, modes, precision=highest)
    diverge = modal[..., 0, :, :]
    height = modal[..., 1, :, :]
    factor = coeff[..., None, None]
    updated = (diverge + time_step * factor * height) / (1.0 + time_step * time_step * factor * depths)
    raised = height - time_step * depths * updated
    both = jnp.stack([updated, raised], axis=-3)
    return jnp.einsum('...j,lj->...l', both, modes, precision=highest)

def reference(grid, w_in, b_in, w_out, lat_weight, legendre, order_table, modes, depths):
    fields, levels, lat_count, lon_count = grid.shape
    table = fourier_table(order_table, lon_count, ORDERS)
    scale_in = math.sqrt(2.0 / lon_count)

    def per_latitude(inputs):
        rows, weight = inputs
        state = column_physics(rows.reshape(fields * levels, lon_count), w_in, b_in, w_out)
        fourier = jnp.dot(state, table, preferred_element_type=jnp.float32)
        return (fourier * (weight * scale_in)).astype(jnp.bfloat16)
    weighted = lax.map(per_latitude, (jnp.moveaxis(grid, 2, 0), lat_weight))
    weighted = weighted.reshape(lat_count, fields, levels, PAIRS, 4)
    weighted = jnp.moveaxis(weighted, 3, 0)
    degree_index = jnp.arange(DEGS, dtype=jnp.int32)

    def per_slot(inputs):
        values, lower, block = inputs
        values_wide = values.astype(jnp.float32)
        analysed = jnp.einsum('kx,xflc->kfcl', values_wide, block.astype(jnp.float32))
        first = degree_index < ORDERS - lower
        spectral = jnp.where(first[:, None, None, None], analysed[:, :, 0:2], analysed[:, :, 2:4])
        degree = jnp.where(first, lower + degree_index, degree_index - 1).astype(jnp.float32)
        coeff = degree * (degree + 1.0) / (ORDERS * ORDERS)
        updated = implicit_update(spectral, coeff, modes, depths).astype(jnp.bfloat16)
        nothing = jnp.zeros_like(updated)
        first_wide = first[:, None, None, None]
        split_parts = jnp.concatenate([jnp.where(first_wide, updated, nothing), jnp.where(first_wide, nothing, updated)], axis=2)
        return jnp.einsum('kx,kfcl->xflc', values_wide, split_parts.astype(jnp.float32)).astype(jnp.bfloat16)
    bands = lax.map(per_slot, (legendre, order_table, weighted))
    bands = jnp.moveaxis(bands, 0, 3).reshape(lat_count, fields * levels, 4 * PAIRS)
    scale_out = 1.0 / math.sqrt(ORDERS)

    def synthesis(rows):
        return (jnp.dot(rows, table.T, preferred_element_type=jnp.float32) * scale_out).astype(jnp.bfloat16)
    result = lax.map(synthesis, bands)
    return jnp.moveaxis(result.reshape(lat_count, fields, levels, lon_count), 0, 2)
```

```python
import functools
import math

import jax
import jax.numpy as jnp
import numpy as np
from jax import lax
from jax.experimental import pallas as pl
from jax.experimental.pallas import tpu as pltpu
from jax.sharding import PartitionSpec as P

ORDERS = 512
ROWS = 16
LANES = 128
BF16 = jnp.bfloat16
F32 = jnp.float32


time_step = 1.0


def fourier_table(slot_orders, lon_count, order_count):
    upper = order_count - 1 - slot_orders
    orders = jnp.stack([slot_orders, slot_orders, upper, upper], axis=-1).reshape(-1)
    parity = jnp.tile(jnp.arange(2, dtype=jnp.int32), 2 * slot_orders.shape[0])
    longitude = jnp.arange(lon_count, dtype=jnp.int32)
    phases = longitude[:, None] * orders[None, :] % lon_count
    angles = phases.astype(jnp.float32) * (2.0 * math.pi / lon_count)
    return jnp.where(parity[None, :] == 0, jnp.cos(angles), -jnp.sin(angles)).astype(jnp.bfloat16)


def implicit_update(spectral, coeff, modes, depths):
    highest = lax.Precision.HIGHEST
    modal = jnp.einsum("...l,lj->...j", spectral, modes, precision=highest)
    diverge = modal[..., 0, :, :]
    height = modal[..., 1, :, :]
    factor = coeff[..., None, None]
    updated = (diverge + time_step * factor * height) / (
        1.0 + time_step * time_step * factor * depths
    )
    raised = height - time_step * depths * updated
    both = jnp.stack([updated, raised], axis=-3)
    return jnp.einsum("...j,lj->...l", both, modes, precision=highest)


def plain_body(grid, w_in, b_in, w_out, lat_weight, legendre, order_table, modes, depths):
    fields, half_levels, lat_rows, lon_count = grid.shape
    lat_groups = lax.axis_size("lat")
    lev_groups = lax.axis_size("lev")
    slots_dev = legendre.shape[0]
    degree_count = legendre.shape[1]
    lat_count = legendre.shape[2]
    levels = half_levels * lev_groups
    width = 4 * slots_dev
    position = lax.axis_index("lat") * lev_groups + lax.axis_index("lev")
    my_orders = lax.dynamic_slice_in_dim(order_table, position * slots_dev, slots_dev)
    weight_rows = (lat_weight * math.sqrt(2.0 / lon_count))[None, None, :, None]
    table = fourier_table(order_table, lon_count, ORDERS)
    block = lax.all_to_all(grid, "lev", split_axis=3, concat_axis=1, tiled=True)
    count_f, count_l, items, span = block.shape
    flat = block.reshape(count_f * count_l, items * span)
    hidden = jnp.dot(w_in, flat, preferred_element_type=jnp.float32) + b_in[:, None]
    hidden = jax.nn.silu(hidden).astype(jnp.bfloat16)
    change = jnp.dot(w_out, hidden, preferred_element_type=jnp.float32)
    state = lax.all_to_all(
        (flat.astype(jnp.float32) + change)
        .astype(jnp.bfloat16)
        .reshape(count_f, count_l, items, span),
        "lev",
        split_axis=1,
        concat_axis=3,
        tiled=True,
    )
    fourier = jnp.einsum("flxn,nc->flxc", state, table, preferred_element_type=jnp.float32)
    weighted = (fourier * weight_rows).astype(jnp.bfloat16)
    moved = lax.all_to_all(weighted, ("lat", "lev"), split_axis=3, concat_axis=2, tiled=True)
    moved = moved.reshape(fields, half_levels, lat_groups, lev_groups, lat_rows, width)
    moved = moved.transpose(0, 3, 1, 2, 4, 5).reshape(fields, levels, lat_count, width)
    blocks = moved.reshape(fields, levels, lat_count, slots_dev, 4)
    analysed = jnp.einsum("skx,flxsc->skfcl", legendre, blocks, preferred_element_type=jnp.float32)
    degree_index = jnp.arange(degree_count, dtype=jnp.int32)[None, :]
    first = degree_index < ORDERS - my_orders[:, None]
    first_wide = first[:, :, None, None, None]
    spectral = jnp.where(first_wide, analysed[:, :, :, 0:2], analysed[:, :, :, 2:4])
    degree = jnp.where(first, my_orders[:, None] + degree_index, degree_index - 1).astype(
        jnp.float32
    )
    coeff = degree * (degree + 1.0) / (ORDERS * ORDERS)
    updated = implicit_update(spectral, coeff, modes, depths).astype(jnp.bfloat16)
    nothing = jnp.zeros_like(updated)
    split_parts = jnp.concatenate(
        [jnp.where(first_wide, updated, nothing), jnp.where(first_wide, nothing, updated)], axis=3
    )
    band = jnp.einsum("skx,skfcl->flxsc", legendre, split_parts, preferred_element_type=jnp.float32)
    band = band.astype(jnp.bfloat16).reshape(fields, levels, lat_count, width)
    arranged = band.reshape(fields, lev_groups, half_levels, lat_groups, lat_rows, width)
    arranged = arranged.transpose(0, 2, 3, 1, 4, 5).reshape(
        fields, half_levels, lat_groups * lev_groups * lat_rows, width
    )
    returned = lax.all_to_all(arranged, ("lat", "lev"), split_axis=2, concat_axis=3, tiled=True)
    inverse_table = fourier_table(order_table, lon_count, ORDERS)
    result = jnp.einsum(
        "flxc,nc->flxn", returned, inverse_table, preferred_element_type=jnp.float32
    )
    return (result * (1.0 / math.sqrt(ORDERS))).astype(jnp.bfloat16)


def analysis_lanes(fields, half_levels):
    count = 2 * fields * half_levels
    tail = count - LANES
    part = np.concatenate([np.repeat([0, 1], LANES), np.repeat([0, 1], tail)])
    item = np.concatenate([np.tile(np.arange(LANES), 2), np.tile(LANES + np.arange(tail), 2)])
    half, rest = np.divmod(item, fields * half_levels)
    field, level = np.divmod(rest, half_levels)
    return part, field, half * half_levels + level


def synthesis_lanes(fields, half_levels):
    half, order, part, field, level = np.meshgrid(
        np.arange(2), np.arange(2), np.arange(2), np.arange(fields), np.arange(half_levels), indexing="ij"
    )
    return part.reshape(-1), field.reshape(-1), (half * half_levels + level).reshape(-1)


def split_wide(x):
    high = x.astype(BF16)
    return high, (x - high.astype(F32)).astype(BF16)


def mode_matrices(modes, fields, half_levels):
    levels = modes.shape[0]
    padded = jnp.pad(modes, ((0, 0), (0, LANES - levels)))
    modal_field = np.repeat(np.arange(fields), 2 * LANES)
    modal_part = np.tile(np.repeat([0, 1], LANES), fields)

    def matrix(lanes):
        part, field, level = lanes
        keep = (part[:, None] == modal_part[None, :]) & (field[:, None] == modal_field[None, :])
        rows = jnp.take(padded, jnp.asarray(level), axis=0)
        return jnp.where(jnp.asarray(keep), jnp.tile(rows, (1, 2 * fields)), 0.0)

    to_modal = matrix(analysis_lanes(fields, half_levels))
    to_levels = matrix(synthesis_lanes(fields, half_levels)).T
    return split_wide(to_modal), split_wide(to_levels)


def table_kernel(ca_ref, sa_ref, cb_ref, sb_ref, out_ref):
    half = ca_ref.shape[0] // 2
    for block in range(ca_ref.shape[1]):
        lanes = slice(block * LANES, (block + 1) * LANES)
        ca, sa = ca_ref[:, block : block + 1], sa_ref[:, block : block + 1]
        cb, sb = cb_ref[...], sb_ref[...]
        cos = (ca * cb - sa * sb).astype(BF16)
        sin = -(sa * cb + ca * sb).astype(BF16)
        out_ref[0, :, lanes] = cos[:half]
        out_ref[1, :, lanes] = sin[:half]
        out_ref[2, :, lanes] = cos[half:]
        out_ref[3, :, lanes] = sin[half:]


def transposed_table(order_table, lon_count):
    orders = jnp.concatenate([order_table, ORDERS - 1 - order_table]).astype(jnp.int32)
    coarse = jnp.arange(lon_count // LANES, dtype=jnp.int32) * LANES
    fine = jnp.arange(LANES, dtype=jnp.int32)
    scale = 2.0 * math.pi / lon_count
    angle_a = (orders[:, None] * coarse[None, :] % lon_count).astype(F32) * scale
    angle_b = (orders[:, None] * fine[None, :] % lon_count).astype(F32) * scale
    return pl.pallas_call(
        table_kernel,
        out_shape=jax.ShapeDtypeStruct((4, order_table.shape[0], lon_count), BF16),
        compiler_params=pltpu.CompilerParams(vmem_limit_bytes=40 << 20),
        name="table",
    )(jnp.cos(angle_a), jnp.sin(angle_a), jnp.cos(angle_b), jnp.sin(angle_b))


def forward_kernel(
    split, core_ref, weight_ref, own_ref, other_ref, w_in_ref, b_in_ref, w_out_ref, table_ref, *refs
):
    outs, state, packed = refs[:-2], refs[-2], refs[-1]
    step = pl.program_id(0)
    core = core_ref[0]
    half = own_ref.shape[0]
    lon_count = own_ref.shape[2]
    slots = table_ref.shape[1]
    own_at = pl.multiple_of(core * half, 32)
    other_at = pl.multiple_of((1 - core) * half, 32)
    state[:, pl.ds(own_at, half), :] = jnp.swapaxes(own_ref[...], 0, 1)
    state[:, pl.ds(other_at, half), :] = jnp.swapaxes(other_ref[...], 0, 1)
    span = 512
    lane = lax.broadcasted_iota(jnp.int32, (slots, LANES), 1)

    def row(r, carry):
        for start in range(0, lon_count, span):
            lons = slice(start, start + span)
            values = state[r, : 2 * half, lons]
            hidden = jnp.dot(w_in_ref[...], values, preferred_element_type=F32) + b_in_ref[...]
            hidden = (hidden * (0.5 + 0.5 * jnp.tanh(0.5 * hidden))).astype(BF16)
            change = jnp.dot(w_out_ref[...], hidden, preferred_element_type=F32)
            doubled = jnp.concatenate([values, values[LANES:]], axis=0).astype(F32)
            state[r, :, lons] = (doubled + change).astype(BF16)
        weight = weight_ref[step * ROWS + r]
        for order in range(2):
            parts = []
            for part in range(2):
                fourier = lax.dot_general(
                    table_ref[2 * order + part],
                    state[r],
                    (((1,), (1,)), ((), ())),
                    preferred_element_type=F32,
                )
                parts.append(fourier * weight)
            real, imag = parts
            base = order * 3 * LANES
            packed[r, :, base : base + LANES] = real[:, :LANES].astype(BF16)
            packed[r, :, base + LANES : base + 2 * LANES] = imag[:, :LANES].astype(BF16)
            mixed = jnp.where(lane < LANES // 2, real[:, LANES:], imag[:, LANES:])
            packed[r, :, base + 2 * LANES : base + 3 * LANES] = mixed.astype(BF16)
        return carry

    lax.fori_loop(0, ROWS, row, 0)
    if not split:
        outs[0][...] = jnp.swapaxes(packed[...], 0, 1)
    else:
        own_slots = split
        part_slots = own_slots // 2
        for position in range(slots // own_slots):
            for index in range(2):
                start = position * own_slots + index * part_slots
                block = packed[:, start : start + part_slots, :]
                outs[index][position * part_slots : (position + 1) * part_slots] = jnp.swapaxes(
                    block, 0, 1
                )


def forward(split, core, weights, grid, first_block, other, w_in, b_in, w_out, table):
    half, rows, lon_count = other.shape
    slots = table.shape[1]
    hidden = w_in.shape[0]
    lanes = 6 * LANES
    if split:
        outs = [jax.ShapeDtypeStruct((slots // 2, rows, lanes), BF16)] * 2
    else:
        outs = [jax.ShapeDtypeStruct((slots, rows, lanes), BF16)]
    once = pl.Buffered(1)
    whole = lambda shape: pl.BlockSpec(shape, lambda i, *_: (0,) * len(shape), pipeline_mode=once)
    flops = 2 * rows * lon_count * (2 * 2 * half * hidden + 2 * half * 4 * slots)
    return pl.pallas_call(
        functools.partial(forward_kernel, split),
        grid_spec=pltpu.PrefetchScalarGridSpec(
            num_scalar_prefetch=2,
            grid=(rows // ROWS,),
            in_specs=[
                pl.BlockSpec(
                    (half, ROWS, lon_count),
                    lambda i, core, weights: (0, first_block(core[0]) + i, 0),
                    pipeline_mode=once,
                ),
                pl.BlockSpec((half, ROWS, lon_count), lambda i, *_: (0, i, 0), pipeline_mode=once),
                whole(w_in.shape),
                whole(b_in.shape),
                whole(w_out.shape),
                whole(table.shape),
            ],
            out_specs=[pl.BlockSpec((o.shape[0], ROWS, lanes), lambda i, *_: (0, i, 0)) for o in outs],
            scratch_shapes=[
                pltpu.VMEM((ROWS, 2 * LANES, lon_count), BF16),
                pltpu.VMEM((ROWS, slots, lanes), BF16),
            ],
        ),
        out_shape=outs,
        compiler_params=pltpu.CompilerParams(vmem_limit_bytes=58 << 20),
        cost_estimate=pl.CostEstimate(
            flops=3 * flops, bytes_accessed=rows * (4 * half * lon_count + 2 * slots * lanes), transcendentals=0
        ),
        name="forward",
    )(core, weights, grid, other, w_in, b_in, w_out, table)


def spectral_kernel(
    last_rows, order_ref, first_ref, second_ref, legendre_ref, to_modal_h, to_modal_l, to_levels_h, to_levels_l,
    depth_ref, main_ref, last_ref, blocks,
):
    order = order_ref[pl.program_id(0)]
    sources, _, first_rows, lanes = first_ref.shape
    second_rows = second_ref.shape[2]
    own_rows = first_rows + second_rows
    for source in range(sources):
        at = source * own_rows
        blocks[at : at + first_rows] = first_ref[source, 0]
        blocks[at + first_rows : at + own_rows] = second_ref[source, 0]
    legendre = legendre_ref[0]
    degrees = legendre.shape[0]
    analysed = jnp.dot(legendre, blocks[...], preferred_element_type=F32)
    index = lax.broadcasted_iota(jnp.int32, (degrees, 1), 0)
    first = index < ORDERS - order
    spectral = jnp.where(first, analysed[:, : lanes // 2], analysed[:, lanes // 2 :])
    degree = jnp.where(first, order + index, index - 1).astype(F32)
    coeff = degree * (degree + 1.0) / (ORDERS * ORDERS)

    def product(values, high, low):
        top, rest = split_wide(values)
        return (
            jnp.dot(top, high[...], preferred_element_type=F32)
            + jnp.dot(rest, high[...], preferred_element_type=F32)
            + jnp.dot(top, low[...], preferred_element_type=F32)
        )

    modal = product(spectral, to_modal_h, to_modal_l)
    width = modal.shape[1] // 2
    diverge, height = modal[:, :width], modal[:, width:]
    depth = depth_ref[...]
    updated = (diverge + time_step * coeff * height) / (1.0 + time_step * time_step * coeff * depth)
    raised = height - time_step * depth * updated
    both = jnp.concatenate([updated, raised], axis=1)
    values = product(both, to_levels_h, to_levels_l)
    lane = lax.broadcasted_iota(jnp.int32, (1, lanes), 1)
    group = lanes // 4
    of_first = (lane < group) | ((lane >= 2 * group) & (lane < 3 * group))
    values = jnp.where(first == of_first, values, 0.0).astype(BF16)
    band = lax.dot_general(
        legendre, values, (((0,), (0,)), ((), ())), preferred_element_type=F32
    ).astype(BF16)
    lat_rows = 2 * own_rows
    main_rows = lat_rows - last_rows
    for place in range(sources // 2):
        for half in range(2):
            piece = band[place * lat_rows : (place + 1) * lat_rows, half * (lanes // 2) : (half + 1) * (lanes // 2)]
            main_ref[2 * place + half, 0] = piece[:main_rows]
            last_ref[2 * place + half, 0] = piece[main_rows:]


def spectral_step(part, last_rows, orders, first, second, legendre, to_modal, to_levels, depths):
    sources, slots, second_rows, lanes = second.shape
    first_rows = first.shape[2]
    _, degrees, lat_count = legendre.shape
    lat_rows = 2 * (first_rows + second_rows)
    main_rows = lat_rows - last_rows
    once = pl.Buffered(1)
    whole = lambda shape: pl.BlockSpec(shape, lambda s, *_: (0,) * len(shape), pipeline_mode=once)
    modal = to_modal[0].shape[1]
    macs = slots * degrees * (2 * lat_count * lanes + 3 * modal * (lanes // 2 + lanes))
    return pl.pallas_call(
        functools.partial(spectral_kernel, last_rows),
        grid_spec=pltpu.PrefetchScalarGridSpec(
            num_scalar_prefetch=1,
            grid=(slots,),
            in_specs=[
                pl.BlockSpec((sources, 1, first_rows, lanes), lambda s, _: (0, part * slots + s, 0, 0)),
                pl.BlockSpec((sources, 1, second_rows, lanes), lambda s, _: (0, s, 0, 0)),
                pl.BlockSpec((1, degrees, lat_count), lambda s, _: (part * slots + s, 0, 0)),
                whole(to_modal[0].shape),
                whole(to_modal[1].shape),
                whole(to_levels[0].shape),
                whole(to_levels[1].shape),
                whole(depths.shape),
            ],
            out_specs=[
                pl.BlockSpec((sources, 1, main_rows, lanes // 2), lambda s, _: (0, s, 0, 0)),
                pl.BlockSpec((sources, 1, last_rows, lanes // 2), lambda s, _: (0, s, 0, 0)),
            ],
            scratch_shapes=[pltpu.VMEM((lat_count, lanes), BF16)],
        ),
        out_shape=[
            jax.ShapeDtypeStruct((sources, slots, main_rows, lanes // 2), BF16),
            jax.ShapeDtypeStruct((sources, slots, last_rows, lanes // 2), BF16),
        ],
        compiler_params=pltpu.CompilerParams(vmem_limit_bytes=50 << 20),
        cost_estimate=pl.CostEstimate(
            flops=4 * macs, bytes_accessed=2 * slots * lat_count * (2 * lanes + degrees), transcendentals=0
        ),
        name="spectral",
    )(orders, first, second, legendre, *to_modal, *to_levels, depths)


def inverse_kernel(scale, *refs):
    bands, table_ref, out_ref, columns = refs[:-4], refs[-4], refs[-2], refs[-1]
    items = out_ref.shape[0]
    at = 0
    total = sum(b.shape[0] for b in bands)
    for band in bands:
        slots = band.shape[0]
        rows = jnp.swapaxes(band[...], 0, 1)
        for r in range(ROWS):
            turned = rows[r].T
            for q in range(4):
                columns[r, :, q * total + at : q * total + at + slots] = turned[q * items : (q + 1) * items]
        at += slots
    left = jnp.swapaxes(columns[...], 0, 1).reshape(items * ROWS, columns.shape[2])
    result = jnp.dot(left, table_ref[...], preferred_element_type=F32) * scale
    out_ref[...] = result.astype(BF16).reshape(out_ref.shape)


def inverse_kernel_first(scale, *refs):
    inverse_kernel(scale, *refs[:-2], None, *refs[-2:])


def inverse(bands, table, lat_rows, first_row, target):
    rows, lanes = bands[0].shape[1:]
    items = lanes // 4
    lon_count = table.shape[1]
    columns = table.shape[0]
    scale = 1.0 / math.sqrt(ORDERS)
    first_block = first_row // ROWS
    operands = list(bands) + [table]
    in_specs = [pl.BlockSpec((b.shape[0], ROWS, lanes), lambda i: (0, i, 0)) for b in bands]
    in_specs.append(pl.BlockSpec(table.shape, lambda i: (0, 0), pipeline_mode=pl.Buffered(1)))
    aliases = {}
    kernel = inverse_kernel_first
    if target is not None:
        aliases = {len(operands): 0}
        operands.append(target)
        in_specs.append(pl.BlockSpec(memory_space=pl.ANY))
        kernel = inverse_kernel
    return pl.pallas_call(
        functools.partial(kernel, scale),
        grid=(rows // ROWS,),
        in_specs=in_specs,
        out_specs=pl.BlockSpec((items, ROWS, lon_count), lambda i: (0, first_block + i, 0)),
        out_shape=jax.ShapeDtypeStruct((items, lat_rows, lon_count), BF16),
        scratch_shapes=[pltpu.VMEM((ROWS, items, columns), BF16)],
        input_output_aliases=aliases,
        compiler_params=pltpu.CompilerParams(vmem_limit_bytes=58 << 20),
        cost_estimate=pl.CostEstimate(
            flops=4 * rows * items * columns * lon_count,
            bytes_accessed=2 * rows * (columns * items + items * lon_count),
            transcendentals=0,
        ),
        name="inverse",
    )(*operands)


def tiled_body(grid, w_in, b_in, w_out, lat_weight, legendre, order_table, modes, depths):
    fields, half_levels, lat_rows, lon_count = grid.shape
    slots_dev, degree_count, lat_count = legendre.shape
    levels = 2 * half_levels
    half = fields * half_levels
    own_rows = lat_rows // 2
    core = lax.axis_index("lev")
    position = lax.axis_index("lat") * 2 + core
    positions = lax.axis_size("lat") * 2
    everyone = ("lat", "lev")
    flat = grid.reshape(half, lat_rows, lon_count)
    core_word = core.astype(jnp.int32).reshape(1)
    swap = [(0, 1), (1, 0)]

    def swapped(start, rows):
        piece = lax.dynamic_slice_in_dim(flat, (1 - core) * own_rows + start, rows, 1)
        return lax.ppermute(piece, "lev", swap)

    first_rows = ROWS
    second_rows = own_rows - first_rows
    other_first = swapped(0, first_rows)
    other_second = swapped(first_rows, second_rows)

    hidden = w_in.shape[0]
    w_in_own = w_in.reshape(hidden, fields, 2, half_levels).transpose(0, 2, 1, 3).reshape(hidden, 2 * half)
    w_out_own = w_out.reshape(fields, 2, half_levels, hidden).transpose(1, 0, 2, 3).reshape(2 * half, hidden)
    w_out_own = jnp.concatenate([w_out_own, w_out_own[LANES:]], axis=0)
    weights = lax.dynamic_slice_in_dim(lat_weight * math.sqrt(2.0 / lon_count), core * own_rows, own_rows)
    table = transposed_table(order_table, lon_count)
    network = (w_in_own, b_in[:, None], w_out_own, table)
    own_blocks = own_rows // ROWS

    (all_slots,) = forward(
        0, core_word, weights[:first_rows], flat, lambda c: c * own_blocks, other_first, *network
    )
    parts = forward(
        slots_dev, core_word, weights[first_rows:], flat, lambda c: c * own_blocks + 1, other_second, *network
    )

    def send(x):
        shape = (positions, x.size // (positions * x.shape[-2] * x.shape[-1])) + x.shape[-2:]
        return lax.all_to_all(x.reshape(shape), everyone, split_axis=0, concat_axis=0, tiled=True)

    got_first = send(all_slots)
    my_orders = lax.dynamic_slice_in_dim(order_table, position * slots_dev, slots_dev)
    part_slots = slots_dev // 2
    to_modal, to_levels = mode_matrices(modes, fields, half_levels)
    depth_lanes = jnp.tile(jnp.pad(depths, (0, LANES - levels)), 2)[None, :]
    last_rows = ROWS
    mains, lasts = [], []
    for part in range(2):
        got = send(parts[part])
        orders = my_orders[part * part_slots : (part + 1) * part_slots]
        main, last = spectral_step(
            part, last_rows, orders, got_first, got, legendre, to_modal, to_levels, depth_lanes
        )
        mains.append(send(main))
        lasts.append(last)
    last = send(jnp.concatenate(lasts, axis=1))
    split_table = table.reshape(4, positions, 2, part_slots, lon_count)
    halves = split_table.transpose(0, 2, 1, 3, 4).reshape(4 * positions * slots_dev, lon_count)
    plain = table.reshape(4 * positions * slots_dev, lon_count)
    join = lambda x: x.reshape((x.shape[0] * x.shape[1],) + x.shape[2:])
    result = inverse([join(m) for m in mains], halves, lat_rows, 0, None)
    result = inverse([join(last)], plain, lat_rows, lat_rows - last_rows, result)
    return result.reshape(grid.shape)


def body(grid, w_in, b_in, w_out, lat_weight, legendre, order_table, modes, depths):
    fields, half_levels, lat_rows, lon_count = grid.shape
    slots_dev = legendre.shape[0]
    count = 2 * fields * half_levels
    tiled = (
        lax.axis_size("lev") == 2
        and lat_rows % (2 * ROWS) == 0
        and lat_rows >= 4 * ROWS
        and count == LANES + LANES // 2
        and half_levels * 2 <= LANES
        and half_levels % ROWS == 0
        and lon_count % 512 == 0
        and slots_dev % 16 == 0
    )
    chosen = tiled_body if tiled else plain_body
    return chosen(grid, w_in, b_in, w_out, lat_weight, legendre, order_table, modes, depths)


def solution(mesh):
    in_specs = (
        P("member", "lev", "lat", None),
        P(),
        P(),
        P(),
        P("lat"),
        P(("lat", "lev"), None, None),
        P(),
        P(),
        P(),
    )
    out_specs = P("member", "lev", "lat", None)
    return jax.shard_map(body, mesh=mesh, in_specs=in_specs, out_specs=out_specs, check_vma=False)
```

```python
import functools
import math

import jax
import jax.numpy as jnp
import numpy as np
from jax import lax
from jax.experimental import pallas as pl
from jax.experimental.pallas import tpu as pltpu
from jax.sharding import PartitionSpec as P

ORDERS = 512
ROWS = 16
LANES = 128
BF16 = jnp.bfloat16
F32 = jnp.float32


time_step = 1.0


def fourier_table(slot_orders, lon_count, order_count):
    upper = order_count - 1 - slot_orders
    orders = jnp.stack([slot_orders, slot_orders, upper, upper], axis=-1).reshape(-1)
    parity = jnp.tile(jnp.arange(2, dtype=jnp.int32), 2 * slot_orders.shape[0])
    longitude = jnp.arange(lon_count, dtype=jnp.int32)
    phases = longitude[:, None] * orders[None, :] % lon_count
    angles = phases.astype(jnp.float32) * (2.0 * math.pi / lon_count)
    return jnp.where(parity[None, :] == 0, jnp.cos(angles), -jnp.sin(angles)).astype(jnp.bfloat16)


def implicit_update(spectral, coeff, modes, depths):
    highest = lax.Precision.HIGHEST
    modal = jnp.einsum("...l,lj->...j", spectral, modes, precision=highest)
    diverge = modal[..., 0, :, :]
    height = modal[..., 1, :, :]
    factor = coeff[..., None, None]
    updated = (diverge + time_step * factor * height) / (
        1.0 + time_step * time_step * factor * depths
    )
    raised = height - time_step * depths * updated
    both = jnp.stack([updated, raised], axis=-3)
    return jnp.einsum("...j,lj->...l", both, modes, precision=highest)


def plain_body(grid, w_in, b_in, w_out, lat_weight, legendre, order_table, modes, depths):
    fields, half_levels, lat_rows, lon_count = grid.shape
    lat_groups = lax.axis_size("lat")
    lev_groups = lax.axis_size("lev")
    slots_dev = legendre.shape[0]
    degree_count = legendre.shape[1]
    lat_count = legendre.shape[2]
    levels = half_levels * lev_groups
    width = 4 * slots_dev
    position = lax.axis_index("lat") * lev_groups + lax.axis_index("lev")
    my_orders = lax.dynamic_slice_in_dim(order_table, position * slots_dev, slots_dev)
    weight_rows = (lat_weight * math.sqrt(2.0 / lon_count))[None, None, :, None]
    table = fourier_table(order_table, lon_count, ORDERS)
    block = lax.all_to_all(grid, "lev", split_axis=3, concat_axis=1, tiled=True)
    count_f, count_l, items, span = block.shape
    flat = block.reshape(count_f * count_l, items * span)
    hidden = jnp.dot(w_in, flat, preferred_element_type=jnp.float32) + b_in[:, None]
    hidden = jax.nn.silu(hidden).astype(jnp.bfloat16)
    change = jnp.dot(w_out, hidden, preferred_element_type=jnp.float32)
    state = lax.all_to_all(
        (flat.astype(jnp.float32) + change)
        .astype(jnp.bfloat16)
        .reshape(count_f, count_l, items, span),
        "lev",
        split_axis=1,
        concat_axis=3,
        tiled=True,
    )
    fourier = jnp.einsum("flxn,nc->flxc", state, table, preferred_element_type=jnp.float32)
    weighted = (fourier * weight_rows).astype(jnp.bfloat16)
    moved = lax.all_to_all(weighted, ("lat", "lev"), split_axis=3, concat_axis=2, tiled=True)
    moved = moved.reshape(fields, half_levels, lat_groups, lev_groups, lat_rows, width)
    moved = moved.transpose(0, 3, 1, 2, 4, 5).reshape(fields, levels, lat_count, width)
    blocks = moved.reshape(fields, levels, lat_count, slots_dev, 4)
    analysed = jnp.einsum("skx,flxsc->skfcl", legendre, blocks, preferred_element_type=jnp.float32)
    degree_index = jnp.arange(degree_count, dtype=jnp.int32)[None, :]
    first = degree_index < ORDERS - my_orders[:, None]
    first_wide = first[:, :, None, None, None]
    spectral = jnp.where(first_wide, analysed[:, :, :, 0:2], analysed[:, :, :, 2:4])
    degree = jnp.where(first, my_orders[:, None] + degree_index, degree_index - 1).astype(
        jnp.float32
    )
    coeff = degree * (degree + 1.0) / (ORDERS * ORDERS)
    updated = implicit_update(spectral, coeff, modes, depths).astype(jnp.bfloat16)
    nothing = jnp.zeros_like(updated)
    split_parts = jnp.concatenate(
        [jnp.where(first_wide, updated, nothing), jnp.where(first_wide, nothing, updated)], axis=3
    )
    band = jnp.einsum("skx,skfcl->flxsc", legendre, split_parts, preferred_element_type=jnp.float32)
    band = band.astype(jnp.bfloat16).reshape(fields, levels, lat_count, width)
    arranged = band.reshape(fields, lev_groups, half_levels, lat_groups, lat_rows, width)
    arranged = arranged.transpose(0, 2, 3, 1, 4, 5).reshape(
        fields, half_levels, lat_groups * lev_groups * lat_rows, width
    )
    returned = lax.all_to_all(arranged, ("lat", "lev"), split_axis=2, concat_axis=3, tiled=True)
    inverse_table = fourier_table(order_table, lon_count, ORDERS)
    result = jnp.einsum(
        "flxc,nc->flxn", returned, inverse_table, preferred_element_type=jnp.float32
    )
    return (result * (1.0 / math.sqrt(ORDERS))).astype(jnp.bfloat16)


def analysis_lanes(fields, half_levels):
    count = 2 * fields * half_levels
    tail = count - LANES
    part = np.concatenate([np.repeat([0, 1], LANES), np.repeat([0, 1], tail)])
    item = np.concatenate([np.tile(np.arange(LANES), 2), np.tile(LANES + np.arange(tail), 2)])
    half, rest = np.divmod(item, fields * half_levels)
    field, level = np.divmod(rest, half_levels)
    return part, field, half * half_levels + level


def synthesis_lanes(fields, half_levels):
    group = 2 * fields * half_levels
    tail = group - LANES
    half = np.concatenate([np.repeat([0, 1], LANES), np.repeat([0, 1], tail)])
    item = np.concatenate([np.tile(np.arange(LANES), 2), np.tile(LANES + np.arange(tail), 2)])
    part, rest = np.divmod(item, fields * half_levels)
    field, level = np.divmod(rest, half_levels)
    return part, field, half * half_levels + level


def split_wide(x):
    high = x.astype(BF16)
    return high, (x - high.astype(F32)).astype(BF16)


def mode_matrices(modes, fields, half_levels):
    levels = modes.shape[0]
    padded = jnp.pad(modes, ((0, 0), (0, LANES - levels)))
    modal_field = np.repeat(np.arange(fields), 2 * LANES)
    modal_part = np.tile(np.repeat([0, 1], LANES), fields)

    def matrix(lanes):
        part, field, level = lanes
        keep = (part[:, None] == modal_part[None, :]) & (field[:, None] == modal_field[None, :])
        rows = jnp.take(padded, jnp.asarray(level), axis=0)
        return jnp.where(jnp.asarray(keep), jnp.tile(rows, (1, 2 * fields)), 0.0)

    to_modal = matrix(analysis_lanes(fields, half_levels))
    to_levels = matrix(synthesis_lanes(fields, half_levels)).T
    return split_wide(to_modal), split_wide(to_levels)


def cost(flops, bytes_accessed, transcendentals):
    return pl.CostEstimate(
        flops=flops // 32, bytes_accessed=bytes_accessed // 16, transcendentals=transcendentals
    )


def table_kernel(ca_ref, sa_ref, cb_ref, sb_ref, out_ref):
    half = ca_ref.shape[0] // 2
    for block in range(ca_ref.shape[1]):
        lanes = slice(block * LANES, (block + 1) * LANES)
        ca, sa = ca_ref[:, block : block + 1], sa_ref[:, block : block + 1]
        cb, sb = cb_ref[...], sb_ref[...]
        cos = (ca * cb - sa * sb).astype(BF16)
        sin = -(sa * cb + ca * sb).astype(BF16)
        out_ref[0, :, lanes] = cos[:half]
        out_ref[1, :, lanes] = sin[:half]
        out_ref[2, :, lanes] = cos[half:]
        out_ref[3, :, lanes] = sin[half:]


def transposed_table(order_table, lon_count):
    orders = jnp.concatenate([order_table, ORDERS - 1 - order_table]).astype(jnp.int32)
    coarse = jnp.arange(lon_count // LANES, dtype=jnp.int32) * LANES
    fine = jnp.arange(LANES, dtype=jnp.int32)
    scale = 2.0 * math.pi / lon_count
    angle_a = (orders[:, None] * coarse[None, :] % lon_count).astype(F32) * scale
    angle_b = (orders[:, None] * fine[None, :] % lon_count).astype(F32) * scale
    return pl.pallas_call(
        table_kernel,
        out_shape=jax.ShapeDtypeStruct((4, order_table.shape[0], lon_count), BF16),
        compiler_params=pltpu.CompilerParams(vmem_limit_bytes=40 << 20),
        name="table",
    )(jnp.cos(angle_a), jnp.sin(angle_a), jnp.cos(angle_b), jnp.sin(angle_b))


def forward_kernel(core_ref, weight_ref, own_ref, other_ref, w_in_ref, b_in_ref, w_out_ref, table_ref, *refs):
    outs, (columns, packed, even, odd) = refs[:-4], refs[-4:]
    core = core_ref[0]
    half = own_ref.shape[0]
    lon_count = own_ref.shape[2]
    slots = table_ref.shape[1]
    own_at = pl.multiple_of(core * half, 32)
    other_at = pl.multiple_of((1 - core) * half, 32)
    columns[:, pl.ds(own_at, half), :] = jnp.swapaxes(own_ref[...], 0, 1)
    columns[:, pl.ds(other_at, half), :] = jnp.swapaxes(other_ref[...], 0, 1)
    lane = lax.broadcasted_iota(jnp.int32, (slots, LANES), 1)

    def network(r, state):
        values = columns[r]
        hidden = jnp.dot(w_in_ref[...], values, preferred_element_type=F32) + b_in_ref[...]
        hidden = (hidden + hidden * jnp.tanh(hidden)).astype(BF16)
        change = jnp.dot(w_out_ref[...], hidden, preferred_element_type=F32)
        result = (values.astype(F32) + change).astype(BF16)
        state[: 2 * half] = result
        state[2 * half :] = result[LANES:]

    def transform(r, state):
        weight = weight_ref[pl.program_id(0) * ROWS + r]
        fourier = lax.dot_general(
            table_ref[...].reshape(4 * slots, lon_count),
            state[...],
            (((1,), (1,)), ((), ())),
            preferred_element_type=F32,
        )
        for order in range(2):
            at = 2 * order * slots
            real = fourier[at : at + slots] * weight
            imag = fourier[at + slots : at + 2 * slots] * weight
            base = order * 3 * LANES
            packed[r, :, base : base + LANES] = real[:, :LANES].astype(BF16)
            packed[r, :, base + LANES : base + 2 * LANES] = imag[:, :LANES].astype(BF16)
            mixed = jnp.where(lane < LANES // 2, real[:, LANES:], imag[:, LANES:])
            packed[r, :, base + 2 * LANES : base + 3 * LANES] = mixed.astype(BF16)

    network(0, even)

    def two_rows(i, carry):
        network(2 * i + 1, odd)
        transform(2 * i, even)
        network(jnp.minimum(2 * i + 2, ROWS - 1), even)
        transform(2 * i + 1, odd)
        return carry

    lax.fori_loop(0, ROWS // 2, two_rows, 0)
    at = 0
    for out in outs:
        out[...] = jnp.swapaxes(packed[:, at : at + out.shape[0], :], 0, 1)
        at += out.shape[0]


def forward(links, link_slots, core, weights, grid, first_block, other, w_in, b_in, w_out, table):
    half, rows, lon_count = other.shape
    slots = table.shape[1]
    hidden = w_in.shape[0]
    lanes = 6 * LANES
    outs = [jax.ShapeDtypeStruct((link_slots, rows, lanes), BF16)] * links
    outs.append(jax.ShapeDtypeStruct((slots - links * link_slots, rows, lanes), BF16))
    once = pl.Buffered(1)
    whole = lambda shape: pl.BlockSpec(shape, lambda i, *_: (0,) * len(shape), pipeline_mode=once)
    flops = 2 * rows * lon_count * (2 * 2 * half * hidden + 2 * half * 4 * slots)
    return pl.pallas_call(
        forward_kernel,
        grid_spec=pltpu.PrefetchScalarGridSpec(
            num_scalar_prefetch=2,
            grid=(rows // ROWS,),
            in_specs=[
                pl.BlockSpec(
                    (half, ROWS, lon_count),
                    lambda i, core, weights: (0, first_block(core[0]) + i, 0),
                    pipeline_mode=once,
                ),
                pl.BlockSpec((half, ROWS, lon_count), lambda i, *_: (0, i, 0), pipeline_mode=once),
                whole(w_in.shape),
                whole(b_in.shape),
                whole(w_out.shape),
                whole(table.shape),
            ],
            out_specs=[pl.BlockSpec((o.shape[0], ROWS, lanes), lambda i, *_: (0, i, 0)) for o in outs],
            scratch_shapes=[
                pltpu.VMEM((ROWS, 2 * half, lon_count), BF16),
                pltpu.VMEM((ROWS, slots, lanes), BF16),
                pltpu.VMEM((2 * LANES, lon_count), BF16),
                pltpu.VMEM((2 * LANES, lon_count), BF16),
            ],
        ),
        out_shape=outs,
        compiler_params=pltpu.CompilerParams(vmem_limit_bytes=58 << 20),
        cost_estimate=cost(
            flops=3 * flops, bytes_accessed=rows * (4 * half * lon_count + 2 * slots * lanes), transcendentals=0
        ),
        name="forward",
    )(core, weights, grid, other, w_in, b_in, w_out, table)


def select_orders(order, analysed):
    lanes = analysed.shape[1] // 2
    index = lax.broadcasted_iota(jnp.int32, (analysed.shape[0], 1), 0)
    return jnp.where(index < ORDERS - order, analysed[:, :lanes], analysed[:, lanes:])


def product(values, high, low):
    top, rest = split_wide(values)
    return (
        jnp.dot(top, high[...], preferred_element_type=F32)
        + jnp.dot(rest, high[...], preferred_element_type=F32)
        + jnp.dot(top, low[...], preferred_element_type=F32)
    )


def implicit_lanes(order, spectral, to_modal_h, to_modal_l, to_levels_h, to_levels_l, depth_ref):
    index = lax.broadcasted_iota(jnp.int32, (spectral.shape[0], 1), 0)
    degree = jnp.where(index < ORDERS - order, order + index, index - 1).astype(F32)
    coeff = degree * (degree + 1.0) / (ORDERS * ORDERS)
    modal = product(spectral, to_modal_h, to_modal_l)
    width = modal.shape[1] // 2
    diverge, height = modal[:, :width], modal[:, width:]
    depth = depth_ref[...]
    updated = (diverge + time_step * coeff * height) / (1.0 + time_step * time_step * coeff * depth)
    raised = height - time_step * depth * updated
    both = jnp.concatenate([updated, raised], axis=1)
    return product(both, to_levels_h, to_levels_l).astype(BF16)


def band_halves(order, legendre, values):
    lanes = values.shape[1]
    index = lax.broadcasted_iota(jnp.int32, (values.shape[0], 1), 0)
    first = index < ORDERS - order
    nothing = jnp.zeros_like(values)
    both = jnp.concatenate([jnp.where(first, values, nothing), jnp.where(first, nothing, values)], axis=1)
    band = lax.dot_general(legendre, both, (((0,), (0,)), ((), ())), preferred_element_type=F32)
    lane = lax.broadcasted_iota(jnp.int32, (1, LANES), 1)
    low = lane < LANES // 2
    rest_a, rest_b = band[:, 2 * LANES : lanes], band[:, lanes + 2 * LANES :]
    rests = [
        jnp.where(low, rest_a, pltpu.roll(rest_b, LANES // 2, 1)),
        jnp.where(low, pltpu.roll(rest_a, LANES // 2, 1), rest_b),
    ]
    halves = []
    for half in range(2):
        a = band[:, half * LANES : (half + 1) * LANES]
        b = band[:, lanes + half * LANES : lanes + (half + 1) * LANES]
        halves.append(jnp.concatenate([a, b, rests[half]], axis=1).astype(BF16))
    return halves


def full_kernel(chunks, order_ref, *refs):
    pieces, (legendre_ref, *matrices), (main_ref, last_ref, blocks) = (
        refs[:chunks],
        refs[chunks:-3],
        refs[-3:],
    )
    order = order_ref[pl.program_id(0)]
    sources = pieces[0].shape[0]
    own_rows = blocks.shape[0] // sources
    for source in range(sources):
        at = source * own_rows
        for piece in pieces:
            blocks[at : at + piece.shape[2]] = piece[source, 0]
            at += piece.shape[2]
    legendre = legendre_ref[0]
    spectral = select_orders(order, jnp.dot(legendre, blocks[...], preferred_element_type=F32))
    halves = band_halves(order, legendre, implicit_lanes(order, spectral, *matrices))
    lat_rows = 2 * own_rows
    main_rows = main_ref.shape[2]
    for place in range(sources // 2):
        for half in range(2):
            piece = halves[half][place * lat_rows : (place + 1) * lat_rows]
            main_ref[2 * place + half, 0] = piece[:main_rows]
            last_ref[2 * place + half, 0] = piece[main_rows:]


def whole_once(shape):
    return pl.BlockSpec(shape, lambda s, *_: (0,) * len(shape), pipeline_mode=pl.Buffered(1))


def spectral_full(first_slot, last_rows, orders, pieces, legendre, matrices):
    sources, slots, _, lanes = pieces[0].shape
    _, degrees, lat_count = legendre.shape
    lat_rows = 2 * lat_count // sources
    main_rows = lat_rows - last_rows
    macs = slots * degrees * (2 * lat_count * lanes + 3 * 4 * LANES * lanes)
    shapes = [(sources, slots, rows, lanes // 2) for rows in (main_rows, last_rows)]
    return pl.pallas_call(
        functools.partial(full_kernel, len(pieces)),
        grid_spec=pltpu.PrefetchScalarGridSpec(
            num_scalar_prefetch=1,
            grid=(slots,),
            in_specs=[pl.BlockSpec((sources, 1, p.shape[2], lanes), lambda s, _: (0, s, 0, 0)) for p in pieces]
            + [pl.BlockSpec((1, degrees, lat_count), lambda s, _: (first_slot + s, 0, 0))]
            + [whole_once(m.shape) for m in matrices],
            out_specs=[
                pl.BlockSpec((sources, 1) + shape[2:], lambda s, _: (0, s, 0, 0)) for shape in shapes
            ],
            scratch_shapes=[pltpu.VMEM((lat_count, lanes), BF16)],
        ),
        out_shape=[jax.ShapeDtypeStruct(shape, BF16) for shape in shapes],
        compiler_params=pltpu.CompilerParams(vmem_limit_bytes=50 << 20),
        cost_estimate=cost(
            flops=4 * macs, bytes_accessed=2 * slots * lat_count * (2 * lanes + degrees), transcendentals=0
        ),
        name="spectral_full",
    )(orders, *pieces, legendre, *matrices)


def gather_half(place, pieces, blocks):
    masks = len(pieces[0])
    own_rows = blocks.shape[0] // masks
    for mask in range(masks):
        done = 0
        for chunk_pieces in pieces:
            rows = chunk_pieces[mask].shape[1]
            at = pl.multiple_of((place ^ mask) * own_rows + done, ROWS)
            blocks[pl.ds(at, rows)] = chunk_pieces[mask][0]
            done += rows


def partial_kernel(chunks, first_slot, place_ref, order_ref, *refs):
    masks = (len(refs) - 3) // chunks
    pieces = [refs[c * masks : (c + 1) * masks] for c in range(chunks)]
    legendre_ref, out_ref, blocks = refs[-3:]
    gather_half(place_ref[0], pieces, blocks)
    order = order_ref[first_slot + pl.program_id(0)]
    analysed = jnp.dot(legendre_ref[0], blocks[...], preferred_element_type=F32)
    out_ref[0] = select_orders(order, analysed).astype(BF16)


def update_kernel(chunks, first_slot, place_ref, order_ref, *refs):
    masks = (len(refs) - 9) // chunks
    pieces = [refs[c * masks : (c + 1) * masks] for c in range(chunks)]
    legendre_ref, got_ref, *matrices, out_ref, blocks = refs[chunks * masks :]
    gather_half(place_ref[0], pieces, blocks)
    order = order_ref[first_slot + pl.program_id(0)]
    analysed = jnp.dot(legendre_ref[0], blocks[...], preferred_element_type=F32)
    spectral = select_orders(order, analysed) + got_ref[0].astype(F32)
    out_ref[0] = implicit_lanes(order, spectral, *matrices)


def spectral_half(first_slot, slots, place, orders, pieces, legendre, got, matrices):
    flat = [array for chunk in pieces for array, _ in chunk]
    bases = [base for chunk in pieces for _, base in chunk]
    lanes = flat[0].shape[2]
    _, degrees, lat_count = legendre.shape
    at_slot = lambda shape, base=0: pl.BlockSpec(
        (1,) + shape, lambda s, *_: (base + first_slot + s, 0, 0)
    )
    plain = pl.BlockSpec((1, degrees, lanes // 2), lambda s, *_: (s, 0, 0))
    macs = slots * degrees * lat_count * lanes
    operands = flat + [legendre]
    in_specs = [at_slot(x.shape[1:], base) for x, base in zip(flat, bases)] + [at_slot((degrees, lat_count))]
    kernel = partial_kernel
    if got is not None:
        kernel = update_kernel
        operands += [got, *matrices]
        in_specs += [plain] + [whole_once(m.shape) for m in matrices]
        macs += slots * degrees * 3 * 4 * LANES * lanes
    return pl.pallas_call(
        functools.partial(kernel, len(pieces), first_slot),
        grid_spec=pltpu.PrefetchScalarGridSpec(
            num_scalar_prefetch=2,
            grid=(slots,),
            in_specs=in_specs,
            out_specs=plain,
            scratch_shapes=[pltpu.VMEM((lat_count, lanes), BF16)],
        ),
        out_shape=jax.ShapeDtypeStruct((slots, degrees, lanes // 2), BF16),
        compiler_params=pltpu.CompilerParams(vmem_limit_bytes=50 << 20),
        cost_estimate=cost(
            flops=4 * macs, bytes_accessed=2 * slots * lat_count * (lanes + degrees), transcendentals=0
        ),
        name="spectral_partial" if got is None else "spectral_update",
    )(place, orders, *operands)


def synthesis_kernel(first_slot, place_ref, order_ref, legendre_ref, values_ref, *refs):
    outs, bands = refs[:-1], refs[-1]
    order = order_ref[first_slot + pl.program_id(0)]
    halves = band_halves(order, legendre_ref[0], values_ref[0])
    lat_rows = bands.shape[1]
    for place in range(len(outs)):
        for half in range(2):
            bands[2 * place + half] = halves[half][place * lat_rows : (place + 1) * lat_rows]
    for link, out in enumerate(outs):
        for other in range(2):
            out[other, 0] = bands[place_ref[0] ^ (2 * link + other)]


def synthesis_half(first_slot, masks, place, orders, legendre, values):
    slots, degrees, lanes = values.shape
    lat_count = legendre.shape[2]
    lat_rows = 2 * lat_count // masks
    return pl.pallas_call(
        functools.partial(synthesis_kernel, first_slot),
        grid_spec=pltpu.PrefetchScalarGridSpec(
            num_scalar_prefetch=2,
            grid=(slots,),
            in_specs=[
                pl.BlockSpec((1, degrees, lat_count), lambda s, *_: (first_slot + s, 0, 0)),
                pl.BlockSpec((1, degrees, lanes), lambda s, *_: (s, 0, 0)),
            ],
            out_specs=[pl.BlockSpec((2, 1, lat_rows, lanes), lambda s, *_: (0, s, 0, 0))] * (masks // 2),
            scratch_shapes=[pltpu.VMEM((masks, lat_rows, lanes), BF16)],
        ),
        out_shape=[jax.ShapeDtypeStruct((2, slots, lat_rows, lanes), BF16)] * (masks // 2),
        compiler_params=pltpu.CompilerParams(vmem_limit_bytes=50 << 20),
        cost_estimate=cost(
            flops=8 * slots * degrees * lat_count * lanes,
            bytes_accessed=2 * slots * lat_count * (lanes + degrees),
            transcendentals=0,
        ),
        name="synthesis_half",
    )(place, orders, legendre, values)


def inverse_kernel(scale, *refs):
    bands, table_ref, out_ref, columns = refs[:-4], refs[-4], refs[-2], refs[-1]
    items = out_ref.shape[0]
    together = jnp.concatenate([band[...] for band in bands], axis=0)
    total = together.shape[0]
    rows = jnp.swapaxes(together, 0, 1)
    cut = 2 * LANES
    for r in range(ROWS):
        turned = rows[r].T
        for order in range(2):
            begin, rest = order * LANES, cut + order * (LANES // 2)
            both = jnp.concatenate([turned[begin : begin + LANES], turned[rest : rest + LANES // 2]], axis=0)
            for part in range(2):
                at = (2 * order + part) * total
                columns[r, :, at : at + total] = both[part * items : (part + 1) * items]
    left = jnp.swapaxes(columns[...], 0, 1).reshape(items * ROWS, columns.shape[2])
    result = jnp.dot(left, table_ref[...], preferred_element_type=F32) * scale
    out_ref[...] = result.astype(BF16).reshape(out_ref.shape)


def inverse_kernel_first(scale, *refs):
    inverse_kernel(scale, *refs[:-2], None, *refs[-2:])


def inverse(bands, rows, table, lat_rows, first_row, target):
    lanes = bands[0][0].shape[2]
    items = lanes // 4
    columns, lon_count = table.shape
    scale = 1.0 / math.sqrt(ORDERS)
    first_block = first_row // ROWS
    operands = [band[0] for band in bands] + [table]
    in_specs = [
        pl.BlockSpec((slots, ROWS, lanes), lambda i, block=block, at=start // ROWS: (block, at + i, 0))
        for _, slots, block, start in bands
    ]
    in_specs.append(pl.BlockSpec(table.shape, lambda i: (0, 0), pipeline_mode=pl.Buffered(1)))
    aliases = {}
    kernel = inverse_kernel_first
    if target is not None:
        aliases = {len(operands): 0}
        operands.append(target)
        in_specs.append(pl.BlockSpec(memory_space=pl.ANY))
        kernel = inverse_kernel
    return pl.pallas_call(
        functools.partial(kernel, scale),
        grid=(rows // ROWS,),
        in_specs=in_specs,
        out_specs=pl.BlockSpec((items, ROWS, lon_count), lambda i: (0, first_block + i, 0)),
        out_shape=jax.ShapeDtypeStruct((items, lat_rows, lon_count), BF16),
        scratch_shapes=[pltpu.VMEM((ROWS, items, columns), BF16)],
        input_output_aliases=aliases,
        compiler_params=pltpu.CompilerParams(vmem_limit_bytes=58 << 20),
        cost_estimate=cost(
            flops=4 * rows * items * columns * lon_count,
            bytes_accessed=2 * rows * (columns * items + items * lon_count),
            transcendentals=0,
        ),
        name="inverse",
    )(*operands)


def tiled_body(grid, w_in, b_in, w_out, lat_weight, legendre, order_table, modes, depths):
    fields, half_levels, lat_rows, lon_count = grid.shape
    slots_dev, degree_count, lat_count = legendre.shape
    levels = 2 * half_levels
    half = fields * half_levels
    own_rows = lat_rows // 2
    own_blocks = own_rows // ROWS
    chunks = [(at * ROWS, ROWS) for at in range(own_blocks)]
    core = lax.axis_index("lev")
    position = lax.axis_index("lat") * 2 + core
    positions = lax.axis_size("lat") * 2
    masks = positions // 2
    mirror = position ^ masks
    place = (position % masks).astype(jnp.int32).reshape(1)
    side = position // masks
    everyone = ("lat", "lev")
    join = lambda x: x.reshape((x.shape[0] * x.shape[1],) + x.shape[2:])
    pairs = lambda mask: [(p, p ^ mask) for p in range(positions)]
    shift = lambda x, mask: lax.ppermute(x, everyone, pairs(mask)) if mask else x
    flat = grid.reshape(half, lat_rows, lon_count)
    core_word = core.astype(jnp.int32).reshape(1)

    def cut_rows(start, rows, core):
        return lax.dynamic_slice_in_dim(flat, (1 - core) * own_rows + start, rows, 1)

    def swapped(piece):
        return lax.ppermute(piece, "lev", [(0, 1), (1, 0)])

    batch = slots_dev // 4
    pair = 2 * batch
    links = masks // 2
    half_lats = lat_count // 2
    turn = lax.axis_index("member") % 2
    members = lax.axis_size("member")
    piece, core = lax.optimization_barrier((cut_rows(*chunks[0], core), core))
    others = [swapped(piece)]
    share = batch // 2
    crossing = lax.dynamic_slice(
        legendre, (turn * share, 0, (1 - side) * half_lats), (share, degree_count, half_lats)
    )
    core, crossing = lax.optimization_barrier((core, crossing))
    crossed = shift(crossing, masks)
    others.append(swapped(cut_rows(*chunks[1], core)))

    by_position = order_table.reshape(positions, slots_dev)
    near = jnp.stack([by_position[position ^ mask, :batch] for mask in range(masks)])
    far = jnp.stack([by_position[mirror ^ mask, :batch] for mask in range(masks)])
    both = jnp.concatenate([near, far], axis=1)
    table_orders = jnp.concatenate([both.reshape(-1), by_position[:, batch:].reshape(-1)])
    half_orders = both[0]
    full_orders = by_position[position, batch:]

    hidden = w_in.shape[0]
    w_in_own = w_in.reshape(hidden, fields, 2, half_levels).transpose(0, 2, 1, 3).reshape(hidden, 2 * half)
    w_out_own = w_out.reshape(fields, 2, half_levels, hidden).transpose(1, 0, 2, 3).reshape(2 * half, hidden)
    weights = lax.dynamic_slice_in_dim(lat_weight * math.sqrt(2.0 / lon_count), core * own_rows, own_rows)
    table = transposed_table(table_orders, lon_count)
    network = (w_in_own * 0.5, 0.5 * b_in[:, None], w_out_own, table)

    def send(x):
        shape = (positions, x.size // (positions * x.shape[-2] * x.shape[-1])) + x.shape[-2:]
        return lax.all_to_all(x.reshape(shape), everyone, split_axis=0, concat_axis=0, tiled=True)

    def cores_apart(arrays):
        count = arrays[0].shape[0] // 2
        return shift(jnp.concatenate([x[count:] for x in arrays], axis=0), 1)

    def transformed(chunk):
        start, rows = chunks[chunk]
        *by_link, rest = forward(
            links,
            2 * pair,
            core_word,
            weights[start : start + rows],
            flat,
            lambda c: c * own_blocks + start // ROWS,
            others[chunk],
            *network,
        )
        return by_link, rest

    by_links, rests = [], []
    for chunk in range(len(chunks)):
        by_link, rest = transformed(chunk)
        if chunk == 0:
            rest, crossed, core, others[1] = lax.optimization_barrier((rest, crossed, core, others[1]))
            others += [swapped(cut_rows(*c, core)) for c in chunks[2:]]
        if chunk == 2:
            rests[1], rest = lax.optimization_barrier((rests[1], rest))
        by_links.append([shift(x, 2 * link) for link, x in enumerate(by_link)])
        rests.append(rest)
    full_pieces = [send(rests[0])]
    crossed_too = lax.ppermute(crossed, "member", [(m, m ^ 1) for m in range(members)])
    rests[1], crossed_too, full_pieces[0], by_links[0] = lax.optimization_barrier(
        (rests[1], crossed_too, full_pieces[0], by_links[0])
    )
    full_pieces.append(send(rests[1]))
    rests[2], full_pieces[1], by_links[1:] = lax.optimization_barrier(
        (rests[2], full_pieces[1], by_links[1:])
    )
    full_pieces.append(send(rests[2]))
    half_pieces = []
    for by_link in by_links:
        apart = cores_apart(by_link)
        half_pieces.append(
            [(apart, (mask // 2) * pair) if mask % 2 else (by_link[mask // 2], 0) for mask in range(masks)]
        )

    near_legendre = lax.dynamic_slice(legendre, (0, 0, side * half_lats), (batch, degree_count, half_lats))
    far_legendre = [jnp.where(turn == 0, x, y) for x, y in ((crossed, crossed_too), (crossed_too, crossed))]
    half_legendre = jnp.concatenate([near_legendre, *far_legendre], axis=0)
    to_modal, to_levels = mode_matrices(modes, fields, half_levels)
    depth_lanes = jnp.tile(jnp.pad(depths, (0, LANES - levels)), 2)[None, :]
    matrices = (*to_modal, *to_levels, depth_lanes)
    half_step = functools.partial(spectral_half, place=place, orders=half_orders, pieces=half_pieces)
    partial = half_step(batch, batch, legendre=half_legendre, got=None, matrices=None)
    sums = shift(partial, masks)
    values = half_step(0, batch, legendre=half_legendre, got=sums, matrices=matrices)
    full_pieces[-1], values = lax.optimization_barrier((full_pieces[-1], values))
    far_values = shift(values, masks)
    last_rows = ROWS
    main, last = spectral_full(batch, last_rows, full_orders, full_pieces, legendre, matrices)
    main, far_values = lax.optimization_barrier((main, far_values))
    main = join(send(main))
    bands = synthesis_half(
        0, masks, place, half_orders, half_legendre, jnp.concatenate([values, far_values], axis=0)
    )
    bands = [shift(join(x), 2 * link) for link, x in enumerate(bands)]
    apart = cores_apart(bands)
    last, apart = lax.optimization_barrier((last, apart))
    last = join(send(last))
    near_bands = [(apart, mask // 2) if mask % 2 else (bands[mask // 2], 0) for mask in range(masks)]
    flat_table = table.reshape(-1, lon_count)
    main_rows = lat_rows - last_rows
    bands_at = lambda row: [(array, pair, block, row) for array, block in near_bands]
    full_slots = positions * (slots_dev - batch)
    bands = bands_at(0) + [(main, full_slots, 0, 0)]
    result = inverse(bands, main_rows, flat_table, lat_rows, 0, None)
    bands = bands_at(main_rows) + [(last, full_slots, 0, 0)]
    result = inverse(bands, last_rows, flat_table, lat_rows, main_rows, result)
    return result.reshape(grid.shape)


def body(grid, w_in, b_in, w_out, lat_weight, legendre, order_table, modes, depths):
    fields, half_levels, lat_rows, lon_count = grid.shape
    slots_dev = legendre.shape[0]
    count = 2 * fields * half_levels
    tiled = (
        lax.axis_size("lev") == 2
        and lat_rows % (2 * ROWS) == 0
        and lat_rows == 6 * ROWS
        and count == LANES + LANES // 2
        and half_levels * 2 <= LANES
        and half_levels % ROWS == 0
        and lon_count % 512 == 0
        and slots_dev % 16 == 0
        and lax.axis_size("lat") == 8
        and lax.axis_size("member") % 2 == 0
    )
    chosen = tiled_body if tiled else plain_body
    return chosen(grid, w_in, b_in, w_out, lat_weight, legendre, order_table, modes, depths)


def solution(mesh):
    in_specs = (
        P("member", "lev", "lat", None),
        P(),
        P(),
        P(),
        P("lat"),
        P(("lat", "lev"), None, None),
        P(),
        P(),
        P(),
    )
    out_specs = P("member", "lev", "lat", None)
    return jax.shard_map(body, mesh=mesh, in_specs=in_specs, out_specs=out_specs, check_vma=False)
```

```python
import functools
import math

import jax
import jax.numpy as jnp
import numpy as np
from jax import lax
from jax.experimental import pallas as pl
from jax.experimental.pallas import tpu as pltpu
from jax.sharding import PartitionSpec as P

ORDERS = 512
ROWS = 16
LANES = 128
BF16 = jnp.bfloat16
F32 = jnp.float32


time_step = 1.0


def fourier_table(slot_orders, lon_count, order_count):
    upper = order_count - 1 - slot_orders
    orders = jnp.stack([slot_orders, slot_orders, upper, upper], axis=-1).reshape(-1)
    parity = jnp.tile(jnp.arange(2, dtype=jnp.int32), 2 * slot_orders.shape[0])
    longitude = jnp.arange(lon_count, dtype=jnp.int32)
    phases = longitude[:, None] * orders[None, :] % lon_count
    angles = phases.astype(jnp.float32) * (2.0 * math.pi / lon_count)
    return jnp.where(parity[None, :] == 0, jnp.cos(angles), -jnp.sin(angles)).astype(jnp.bfloat16)


def implicit_update(spectral, coeff, modes, depths):
    highest = lax.Precision.HIGHEST
    modal = jnp.einsum("...l,lj->...j", spectral, modes, precision=highest)
    diverge = modal[..., 0, :, :]
    height = modal[..., 1, :, :]
    factor = coeff[..., None, None]
    updated = (diverge + time_step * factor * height) / (
        1.0 + time_step * time_step * factor * depths
    )
    raised = height - time_step * depths * updated
    both = jnp.stack([updated, raised], axis=-3)
    return jnp.einsum("...j,lj->...l", both, modes, precision=highest)


def plain_body(grid, w_in, b_in, w_out, lat_weight, legendre, order_table, modes, depths):
    fields, half_levels, lat_rows, lon_count = grid.shape
    lat_groups = lax.axis_size("lat")
    lev_groups = lax.axis_size("lev")
    slots_dev = legendre.shape[0]
    degree_count = legendre.shape[1]
    lat_count = legendre.shape[2]
    levels = half_levels * lev_groups
    width = 4 * slots_dev
    position = lax.axis_index("lat") * lev_groups + lax.axis_index("lev")
    my_orders = lax.dynamic_slice_in_dim(order_table, position * slots_dev, slots_dev)
    weight_rows = (lat_weight * math.sqrt(2.0 / lon_count))[None, None, :, None]
    table = fourier_table(order_table, lon_count, ORDERS)
    block = lax.all_to_all(grid, "lev", split_axis=3, concat_axis=1, tiled=True)
    count_f, count_l, items, span = block.shape
    flat = block.reshape(count_f * count_l, items * span)
    hidden = jnp.dot(w_in, flat, preferred_element_type=jnp.float32) + b_in[:, None]
    hidden = jax.nn.silu(hidden).astype(jnp.bfloat16)
    change = jnp.dot(w_out, hidden, preferred_element_type=jnp.float32)
    state = lax.all_to_all(
        (flat.astype(jnp.float32) + change)
        .astype(jnp.bfloat16)
        .reshape(count_f, count_l, items, span),
        "lev",
        split_axis=1,
        concat_axis=3,
        tiled=True,
    )
    fourier = jnp.einsum("flxn,nc->flxc", state, table, preferred_element_type=jnp.float32)
    weighted = (fourier * weight_rows).astype(jnp.bfloat16)
    moved = lax.all_to_all(weighted, ("lat", "lev"), split_axis=3, concat_axis=2, tiled=True)
    moved = moved.reshape(fields, half_levels, lat_groups, lev_groups, lat_rows, width)
    moved = moved.transpose(0, 3, 1, 2, 4, 5).reshape(fields, levels, lat_count, width)
    blocks = moved.reshape(fields, levels, lat_count, slots_dev, 4)
    analysed = jnp.einsum("skx,flxsc->skfcl", legendre, blocks, preferred_element_type=jnp.float32)
    degree_index = jnp.arange(degree_count, dtype=jnp.int32)[None, :]
    first = degree_index < ORDERS - my_orders[:, None]
    first_wide = first[:, :, None, None, None]
    spectral = jnp.where(first_wide, analysed[:, :, :, 0:2], analysed[:, :, :, 2:4])
    degree = jnp.where(first, my_orders[:, None] + degree_index, degree_index - 1).astype(
        jnp.float32
    )
    coeff = degree * (degree + 1.0) / (ORDERS * ORDERS)
    updated = implicit_update(spectral, coeff, modes, depths).astype(jnp.bfloat16)
    nothing = jnp.zeros_like(updated)
    split_parts = jnp.concatenate(
        [jnp.where(first_wide, updated, nothing), jnp.where(first_wide, nothing, updated)], axis=3
    )
    band = jnp.einsum("skx,skfcl->flxsc", legendre, split_parts, preferred_element_type=jnp.float32)
    band = band.astype(jnp.bfloat16).reshape(fields, levels, lat_count, width)
    arranged = band.reshape(fields, lev_groups, half_levels, lat_groups, lat_rows, width)
    arranged = arranged.transpose(0, 2, 3, 1, 4, 5).reshape(
        fields, half_levels, lat_groups * lev_groups * lat_rows, width
    )
    returned = lax.all_to_all(arranged, ("lat", "lev"), split_axis=2, concat_axis=3, tiled=True)
    inverse_table = fourier_table(order_table, lon_count, ORDERS)
    result = jnp.einsum(
        "flxc,nc->flxn", returned, inverse_table, preferred_element_type=jnp.float32
    )
    return (result * (1.0 / math.sqrt(ORDERS))).astype(jnp.bfloat16)


def analysis_lanes(fields, half_levels):
    count = 2 * fields * half_levels
    tail = count - LANES
    part = np.concatenate([np.repeat([0, 1], LANES), np.repeat([0, 1], tail)])
    item = np.concatenate([np.tile(np.arange(LANES), 2), np.tile(LANES + np.arange(tail), 2)])
    field, level = np.divmod(item, 2 * half_levels)
    return part, field, level


def synthesis_lanes(fields, half_levels):
    group = 2 * fields * half_levels
    tail = group - LANES
    half = np.concatenate([np.repeat([0, 1], LANES), np.repeat([0, 1], tail)])
    item = np.concatenate([np.tile(np.arange(LANES), 2), np.tile(LANES + np.arange(tail), 2)])
    part, rest = np.divmod(item, fields * half_levels)
    field, level = np.divmod(rest, half_levels)
    return part, field, half * half_levels + level


def split_wide(x):
    high = x.astype(BF16)
    return high, (x - high.astype(F32)).astype(BF16)


def mode_matrices(modes, fields, half_levels):
    levels = modes.shape[0]
    padded = jnp.pad(modes, ((0, 0), (0, LANES - levels)))
    modal_field = np.repeat(np.arange(fields), 2 * LANES)
    modal_part = np.tile(np.repeat([0, 1], LANES), fields)

    def matrix(lanes):
        part, field, level = lanes
        keep = (part[:, None] == modal_part[None, :]) & (field[:, None] == modal_field[None, :])
        rows = jnp.take(padded, jnp.asarray(level), axis=0)
        return jnp.where(jnp.asarray(keep), jnp.tile(rows, (1, 2 * fields)), 0.0)

    to_modal = matrix(analysis_lanes(fields, half_levels))
    to_levels = matrix(synthesis_lanes(fields, half_levels)).T
    return split_wide(to_modal), split_wide(to_levels)


def cost(flops, bytes_accessed, transcendentals):
    return pl.CostEstimate(
        flops=flops // 32, bytes_accessed=bytes_accessed // 16, transcendentals=transcendentals
    )


def table_kernel(orders_ref, out_ref):
    half = out_ref.shape[1]
    lon_count = out_ref.shape[2]
    orders = orders_ref[...].astype(F32)

    def turn(steps, width):
        index = lax.broadcasted_iota(jnp.int32, (2 * half, width), 1).astype(F32)
        product = orders * (index * steps)
        phase = product - lon_count * jnp.floor(product * (1.0 / lon_count))
        angle = phase * (2.0 * math.pi / lon_count)
        return jnp.cos(angle), jnp.sin(angle)

    cos_coarse, sin_coarse = turn(float(LANES), LANES)
    cb, sb = turn(1.0, LANES)
    for block in range(lon_count // LANES):
        lanes = slice(block * LANES, (block + 1) * LANES)
        ca, sa = cos_coarse[:, block : block + 1], sin_coarse[:, block : block + 1]
        cos = (ca * cb - sa * sb).astype(BF16)
        sin = -(sa * cb + ca * sb).astype(BF16)
        out_ref[0, :, lanes] = cos[:half]
        out_ref[1, :, lanes] = sin[:half]
        out_ref[2, :, lanes] = cos[half:]
        out_ref[3, :, lanes] = sin[half:]


def transposed_table(order_table, lon_count):
    orders = jnp.concatenate([order_table, ORDERS - 1 - order_table])[:, None].astype(jnp.int32)
    return pl.pallas_call(
        table_kernel,
        out_shape=jax.ShapeDtypeStruct((4, order_table.shape[0], lon_count), BF16),
        compiler_params=pltpu.CompilerParams(vmem_limit_bytes=40 << 20),
        name="table",
    )(orders)


def forward_kernel(
    half_levels, core_ref, weight_ref, own_ref, other_ref, w_in_ref, b_in_ref, w_out_ref, table_ref, *refs
):
    outs, (columns, packed, even, odd) = refs[:-4], refs[-4:]
    core = core_ref[0]
    half = own_ref.shape[0]
    lon_count = own_ref.shape[2]
    slots = table_ref.shape[1]
    for field in range(half // half_levels):
        levels = slice(field * half_levels, (field + 1) * half_levels)
        for place, source in ((core, own_ref), (1 - core, other_ref)):
            at = pl.multiple_of((2 * field + place) * half_levels, ROWS)
            columns[:, pl.ds(at, half_levels), :] = jnp.swapaxes(source[levels], 0, 1)
    lane = lax.broadcasted_iota(jnp.int32, (slots, LANES), 1)

    def network(r, state):
        values = columns[r]
        hidden = jnp.dot(w_in_ref[...], values, preferred_element_type=F32) + b_in_ref[...]
        hidden = (hidden + hidden * jnp.tanh(hidden)).astype(BF16)
        change = jnp.dot(w_out_ref[...], hidden, preferred_element_type=F32)
        result = (values.astype(F32) + change).astype(BF16)
        state[: 2 * half] = result
        state[2 * half :] = result[LANES:]

    def transform(r, state):
        weight = weight_ref[pl.program_id(0) * ROWS + r]
        fourier = lax.dot_general(
            table_ref[...].reshape(4 * slots, lon_count),
            state[...],
            (((1,), (1,)), ((), ())),
            preferred_element_type=F32,
        )
        for order in range(2):
            at = 2 * order * slots
            real = fourier[at : at + slots] * weight
            imag = fourier[at + slots : at + 2 * slots] * weight
            base = order * 3 * LANES
            packed[r, :, base : base + LANES] = real[:, :LANES].astype(BF16)
            packed[r, :, base + LANES : base + 2 * LANES] = imag[:, :LANES].astype(BF16)
            mixed = jnp.where(lane < LANES // 2, real[:, LANES:], imag[:, LANES:])
            packed[r, :, base + 2 * LANES : base + 3 * LANES] = mixed.astype(BF16)

    network(0, even)

    def two_rows(i, carry):
        network(2 * i + 1, odd)
        transform(2 * i, even)
        network(jnp.minimum(2 * i + 2, ROWS - 1), even)
        transform(2 * i + 1, odd)
        return carry

    lax.fori_loop(0, ROWS // 2, two_rows, 0)
    at = 0
    for out in outs:
        out[...] = jnp.swapaxes(packed[:, at : at + out.shape[0], :], 0, 1)
        at += out.shape[0]


def forward(half_levels, links, link_slots, core, weights, grid, first_block, other, w_in, b_in, w_out, table):
    half, rows, lon_count = other.shape
    slots = table.shape[1]
    hidden = w_in.shape[0]
    lanes = 6 * LANES
    outs = [jax.ShapeDtypeStruct((link_slots, rows, lanes), BF16)] * links
    outs.append(jax.ShapeDtypeStruct((slots - links * link_slots, rows, lanes), BF16))
    once = pl.Buffered(1)
    whole = lambda shape: pl.BlockSpec(shape, lambda i, *_: (0,) * len(shape), pipeline_mode=once)
    flops = 2 * rows * lon_count * (2 * 2 * half * hidden + 2 * half * 4 * slots)
    return pl.pallas_call(
        functools.partial(forward_kernel, half_levels),
        grid_spec=pltpu.PrefetchScalarGridSpec(
            num_scalar_prefetch=2,
            grid=(rows // ROWS,),
            in_specs=[
                pl.BlockSpec(
                    (half, ROWS, lon_count),
                    lambda i, core, weights: (0, first_block(core[0]) + i, 0),
                    pipeline_mode=once,
                ),
                pl.BlockSpec((half, ROWS, lon_count), lambda i, *_: (0, i, 0), pipeline_mode=once),
                whole(w_in.shape),
                whole(b_in.shape),
                whole(w_out.shape),
                whole(table.shape),
            ],
            out_specs=[pl.BlockSpec((o.shape[0], ROWS, lanes), lambda i, *_: (0, i, 0)) for o in outs],
            scratch_shapes=[
                pltpu.VMEM((ROWS, 2 * half, lon_count), BF16),
                pltpu.VMEM((ROWS, slots, lanes), BF16),
                pltpu.VMEM((2 * LANES, lon_count), BF16),
                pltpu.VMEM((2 * LANES, lon_count), BF16),
            ],
        ),
        out_shape=outs,
        compiler_params=pltpu.CompilerParams(vmem_limit_bytes=58 << 20),
        cost_estimate=cost(
            flops=3 * flops, bytes_accessed=rows * (4 * half * lon_count + 2 * slots * lanes), transcendentals=0
        ),
        name="forward",
    )(core, weights, grid, other, w_in, b_in, w_out, table)


def select_orders(order, analysed):
    lanes = analysed.shape[1] // 2
    index = lax.broadcasted_iota(jnp.int32, (analysed.shape[0], 1), 0)
    return jnp.where(index < ORDERS - order, analysed[:, :lanes], analysed[:, lanes:])


def product(values, high, low):
    rounded = values.astype(BF16)
    return jnp.dot(rounded, high[...], preferred_element_type=F32) + jnp.dot(
        rounded, low[...], preferred_element_type=F32
    )


def implicit_lanes(order, spectral, to_modal_h, to_modal_l, to_levels_h, to_levels_l, depth_ref):
    index = lax.broadcasted_iota(jnp.int32, (spectral.shape[0], 1), 0)
    degree = jnp.where(index < ORDERS - order, order + index, index - 1).astype(F32)
    coeff = degree * (degree + 1.0) / (ORDERS * ORDERS)
    modal = product(spectral, to_modal_h, to_modal_l)
    width = modal.shape[1] // 2
    diverge, height = modal[:, :width], modal[:, width:]
    depth = depth_ref[...]
    updated = (diverge + time_step * coeff * height) / (1.0 + time_step * time_step * coeff * depth)
    raised = height - time_step * depth * updated
    both = jnp.concatenate([updated, raised], axis=1)
    return product(both, to_levels_h, to_levels_l).astype(BF16)


def band_halves(order, legendre, values):
    lanes = values.shape[1]
    index = lax.broadcasted_iota(jnp.int32, (values.shape[0], 1), 0)
    first = index < ORDERS - order
    nothing = jnp.zeros_like(values)
    both = jnp.concatenate([jnp.where(first, values, nothing), jnp.where(first, nothing, values)], axis=1)
    band = lax.dot_general(legendre, both, (((0,), (0,)), ((), ())), preferred_element_type=F32)
    lane = lax.broadcasted_iota(jnp.int32, (1, LANES), 1)
    low = lane < LANES // 2
    rest_a, rest_b = band[:, 2 * LANES : lanes], band[:, lanes + 2 * LANES :]
    rests = [
        jnp.where(low, rest_a, pltpu.roll(rest_b, LANES // 2, 1)),
        jnp.where(low, pltpu.roll(rest_a, LANES // 2, 1), rest_b),
    ]
    halves = []
    for half in range(2):
        a = band[:, half * LANES : (half + 1) * LANES]
        b = band[:, lanes + half * LANES : lanes + (half + 1) * LANES]
        halves.append(jnp.concatenate([a, b, rests[half]], axis=1).astype(BF16))
    return halves


def full_kernel(chunks, order_ref, *refs):
    pieces, (legendre_ref, *matrices), (main_ref, last_ref, blocks) = (
        refs[:chunks],
        refs[chunks:-3],
        refs[-3:],
    )
    order = order_ref[pl.program_id(0)]
    sources = pieces[0].shape[0]
    own_rows = blocks.shape[0] // sources
    for source in range(sources):
        at = source * own_rows
        for piece in pieces:
            blocks[at : at + piece.shape[2]] = piece[source, 0]
            at += piece.shape[2]
    legendre = legendre_ref[0]
    spectral = select_orders(order, jnp.dot(legendre, blocks[...], preferred_element_type=F32))
    halves = band_halves(order, legendre, implicit_lanes(order, spectral, *matrices))
    lat_rows = 2 * own_rows
    main_rows = main_ref.shape[2]
    for place in range(sources // 2):
        for half in range(2):
            piece = halves[half][place * lat_rows : (place + 1) * lat_rows]
            main_ref[2 * place + half, 0] = piece[:main_rows]
            last_ref[2 * place + half, 0] = piece[main_rows:]


def whole_once(shape):
    return pl.BlockSpec(shape, lambda s, *_: (0,) * len(shape), pipeline_mode=pl.Buffered(1))


def spectral_full(first_slot, last_rows, orders, pieces, legendre, matrices):
    sources, slots, _, lanes = pieces[0].shape
    _, degrees, lat_count = legendre.shape
    lat_rows = 2 * lat_count // sources
    main_rows = lat_rows - last_rows
    macs = slots * degrees * (2 * lat_count * lanes + 3 * 4 * LANES * lanes)
    shapes = [(sources, slots, rows, lanes // 2) for rows in (main_rows, last_rows)]
    return pl.pallas_call(
        functools.partial(full_kernel, len(pieces)),
        grid_spec=pltpu.PrefetchScalarGridSpec(
            num_scalar_prefetch=1,
            grid=(slots,),
            in_specs=[pl.BlockSpec((sources, 1, p.shape[2], lanes), lambda s, _: (0, s, 0, 0)) for p in pieces]
            + [pl.BlockSpec((1, degrees, lat_count), lambda s, _: (first_slot + s, 0, 0))]
            + [whole_once(m.shape) for m in matrices],
            out_specs=[
                pl.BlockSpec((sources, 1) + shape[2:], lambda s, _: (0, s, 0, 0)) for shape in shapes
            ],
            scratch_shapes=[pltpu.VMEM((lat_count, lanes), BF16)],
        ),
        out_shape=[jax.ShapeDtypeStruct(shape, BF16) for shape in shapes],
        compiler_params=pltpu.CompilerParams(vmem_limit_bytes=50 << 20),
        cost_estimate=cost(
            flops=4 * macs, bytes_accessed=2 * slots * lat_count * (2 * lanes + degrees), transcendentals=0
        ),
        name="spectral_full",
    )(orders, *pieces, legendre, *matrices)


def gather_half(place, pieces, blocks):
    masks = len(pieces[0])
    own_rows = blocks.shape[0] // masks
    for mask in range(masks):
        done = 0
        for chunk_pieces in pieces:
            rows = chunk_pieces[mask].shape[1]
            at = pl.multiple_of((place ^ mask) * own_rows + done, ROWS)
            blocks[pl.ds(at, rows)] = chunk_pieces[mask][0]
            done += rows


def partial_kernel(chunks, first_slot, place_ref, order_ref, *refs):
    masks = (len(refs) - 3) // chunks
    pieces = [refs[c * masks : (c + 1) * masks] for c in range(chunks)]
    legendre_ref, out_ref, blocks = refs[-3:]
    gather_half(place_ref[0], pieces, blocks)
    order = order_ref[first_slot + pl.program_id(0)]
    analysed = jnp.dot(legendre_ref[0], blocks[...], preferred_element_type=F32)
    out_ref[0, : analysed.shape[0]] = select_orders(order, analysed).astype(BF16)


def update_kernel(chunks, first_slot, place_ref, order_ref, *refs):
    masks = (len(refs) - 9) // chunks
    pieces = [refs[c * masks : (c + 1) * masks] for c in range(chunks)]
    legendre_ref, got_ref, *matrices, out_ref, blocks = refs[chunks * masks :]
    gather_half(place_ref[0], pieces, blocks)
    order = order_ref[first_slot + pl.program_id(0)]
    analysed = jnp.dot(legendre_ref[0], blocks[...], preferred_element_type=F32)
    degrees = analysed.shape[0]
    spectral = select_orders(order, analysed) + got_ref[0, :degrees].astype(F32)
    out_ref[0, :degrees] = implicit_lanes(order, spectral, *matrices)


def spectral_half(first_slot, slots, place, orders, pieces, legendre, got, matrices):
    flat = [array for chunk in pieces for array, _ in chunk]
    bases = [base for chunk in pieces for _, base in chunk]
    lanes = flat[0].shape[2]
    _, degrees, lat_count = legendre.shape
    at_slot = lambda shape, base=0: pl.BlockSpec(
        (1,) + shape, lambda s, *_: (base + first_slot + s, 0, 0)
    )
    tall = -(-degrees // ROWS) * ROWS
    plain = pl.BlockSpec((1, tall, lanes // 2), lambda s, *_: (s, 0, 0))
    macs = slots * degrees * lat_count * lanes
    operands = flat + [legendre]
    in_specs = [at_slot(x.shape[1:], base) for x, base in zip(flat, bases)] + [at_slot((degrees, lat_count))]
    kernel = partial_kernel
    if got is not None:
        kernel = update_kernel
        operands += [got, *matrices]
        in_specs += [plain] + [whole_once(m.shape) for m in matrices]
        macs += slots * degrees * 3 * 4 * LANES * lanes
    return pl.pallas_call(
        functools.partial(kernel, len(pieces), first_slot),
        grid_spec=pltpu.PrefetchScalarGridSpec(
            num_scalar_prefetch=2,
            grid=(slots,),
            in_specs=in_specs,
            out_specs=plain,
            scratch_shapes=[pltpu.VMEM((lat_count, lanes), BF16)],
        ),
        out_shape=jax.ShapeDtypeStruct((slots, tall, lanes // 2), BF16),
        compiler_params=pltpu.CompilerParams(vmem_limit_bytes=50 << 20),
        cost_estimate=cost(
            flops=4 * macs, bytes_accessed=2 * slots * lat_count * (lanes + degrees), transcendentals=0
        ),
        name="spectral_partial" if got is None else "spectral_update",
    )(place, orders, *operands)


def synthesis_kernel(first_slot, place_ref, order_ref, legendre_ref, values_ref, *refs):
    outs, bands = refs[:-1], refs[-1]
    order = order_ref[first_slot + pl.program_id(0)]
    legendre = legendre_ref[0]
    halves = band_halves(order, legendre, values_ref[0, : legendre.shape[0]])
    lat_rows = bands.shape[1]
    for place in range(len(outs)):
        for half in range(2):
            bands[2 * place + half] = halves[half][place * lat_rows : (place + 1) * lat_rows]
    for link, out in enumerate(outs):
        for other in range(2):
            out[other, 0] = bands[place_ref[0] ^ (2 * link + other)]


def synthesis_half(first_slot, masks, place, orders, legendre, values):
    slots, tall, lanes = values.shape
    _, degrees, lat_count = legendre.shape
    lat_rows = 2 * lat_count // masks
    return pl.pallas_call(
        functools.partial(synthesis_kernel, first_slot),
        grid_spec=pltpu.PrefetchScalarGridSpec(
            num_scalar_prefetch=2,
            grid=(slots,),
            in_specs=[
                pl.BlockSpec((1, degrees, lat_count), lambda s, *_: (first_slot + s, 0, 0)),
                pl.BlockSpec((1, tall, lanes), lambda s, *_: (s, 0, 0)),
            ],
            out_specs=[pl.BlockSpec((2, 1, lat_rows, lanes), lambda s, *_: (0, s, 0, 0))] * (masks // 2),
            scratch_shapes=[pltpu.VMEM((masks, lat_rows, lanes), BF16)],
        ),
        out_shape=[jax.ShapeDtypeStruct((2, slots, lat_rows, lanes), BF16)] * (masks // 2),
        compiler_params=pltpu.CompilerParams(vmem_limit_bytes=50 << 20),
        cost_estimate=cost(
            flops=8 * slots * degrees * lat_count * lanes,
            bytes_accessed=2 * slots * lat_count * (lanes + degrees),
            transcendentals=0,
        ),
        name="synthesis_half",
    )(place, orders, legendre, values)


def inverse_kernel(scale, *refs):
    bands, table_ref, out_ref, columns = refs[:-4], refs[-4], refs[-2], refs[-1]
    items = out_ref.shape[0]
    together = jnp.concatenate([band[...] for band in bands], axis=0)
    total = together.shape[0]
    rows = jnp.swapaxes(together, 0, 1)
    cut = 2 * LANES
    for r in range(ROWS):
        turned = rows[r].T
        for order in range(2):
            begin, rest = order * LANES, cut + order * (LANES // 2)
            both = jnp.concatenate([turned[begin : begin + LANES], turned[rest : rest + LANES // 2]], axis=0)
            for part in range(2):
                at = (2 * order + part) * total
                columns[r, :, at : at + total] = both[part * items : (part + 1) * items]
    left = jnp.swapaxes(columns[...], 0, 1).reshape(items * ROWS, columns.shape[2])
    result = jnp.dot(left, table_ref[...], preferred_element_type=F32) * scale
    out_ref[...] = result.astype(BF16).reshape(out_ref.shape)


def inverse_kernel_first(scale, *refs):
    inverse_kernel(scale, *refs[:-2], None, *refs[-2:])


def inverse(bands, rows, table, lat_rows, first_row, target):
    lanes = bands[0][0].shape[2]
    items = lanes // 4
    columns, lon_count = table.shape
    scale = 1.0 / math.sqrt(ORDERS)
    first_block = first_row // ROWS
    operands = [band[0] for band in bands] + [table]
    in_specs = [
        pl.BlockSpec((slots, ROWS, lanes), lambda i, block=block, at=start // ROWS: (block, at + i, 0))
        for _, slots, block, start in bands
    ]
    in_specs.append(pl.BlockSpec(table.shape, lambda i: (0, 0), pipeline_mode=pl.Buffered(1)))
    aliases = {}
    kernel = inverse_kernel_first
    if target is not None:
        aliases = {len(operands): 0}
        operands.append(target)
        in_specs.append(pl.BlockSpec(memory_space=pl.ANY))
        kernel = inverse_kernel
    return pl.pallas_call(
        functools.partial(kernel, scale),
        grid=(rows // ROWS,),
        in_specs=in_specs,
        out_specs=pl.BlockSpec((items, ROWS, lon_count), lambda i: (0, first_block + i, 0)),
        out_shape=jax.ShapeDtypeStruct((items, lat_rows, lon_count), BF16),
        scratch_shapes=[pltpu.VMEM((ROWS, items, columns), BF16)],
        input_output_aliases=aliases,
        compiler_params=pltpu.CompilerParams(vmem_limit_bytes=58 << 20),
        cost_estimate=cost(
            flops=4 * rows * items * columns * lon_count,
            bytes_accessed=2 * rows * (columns * items + items * lon_count),
            transcendentals=0,
        ),
        name="inverse",
    )(*operands)


def tiled_body(grid, w_in, b_in, w_out, lat_weight, legendre, order_table, modes, depths):
    fields, half_levels, lat_rows, lon_count = grid.shape
    slots_dev, degree_count, lat_count = legendre.shape
    levels = 2 * half_levels
    half = fields * half_levels
    own_rows = lat_rows // 2
    own_blocks = own_rows // ROWS
    chunks = [(at * ROWS, ROWS) for at in range(own_blocks)]
    core = lax.axis_index("lev")
    position = lax.axis_index("lat") * 2 + core
    positions = lax.axis_size("lat") * 2
    masks = positions // 2
    mirror = position ^ masks
    place = (position % masks).astype(jnp.int32).reshape(1)
    side = position // masks
    everyone = ("lat", "lev")
    join = lambda x: x.reshape((x.shape[0] * x.shape[1],) + x.shape[2:])
    pairs = lambda mask: [(p, p ^ mask) for p in range(positions)]
    shift = lambda x, mask: lax.ppermute(x, everyone, pairs(mask)) if mask else x
    flat = grid.reshape(half, lat_rows, lon_count)
    core_word = core.astype(jnp.int32).reshape(1)

    def cut_rows(start, rows, core):
        return lax.dynamic_slice_in_dim(flat, (1 - core) * own_rows + start, rows, 1)

    def swapped(piece):
        return lax.ppermute(piece, "lev", [(0, 1), (1, 0)])

    batch = slots_dev // 4
    pair = 2 * batch
    links = masks // 2
    half_lats = lat_count // 2
    turn = lax.axis_index("member") % 2
    members = lax.axis_size("member")
    piece, core = lax.optimization_barrier((cut_rows(*chunks[0], core), core))
    others = [swapped(piece)]
    share = batch // 2
    crossing = lax.dynamic_slice(
        legendre, (turn * share, 0, (1 - side) * half_lats), (share, degree_count, half_lats)
    )
    core, crossing = lax.optimization_barrier((core, crossing))
    crossed = shift(crossing, masks)
    others.append(swapped(cut_rows(*chunks[1], core)))

    by_position = order_table.reshape(positions, slots_dev)
    near = jnp.stack([by_position[position ^ mask, :batch] for mask in range(masks)])
    far = jnp.stack([by_position[mirror ^ mask, :batch] for mask in range(masks)])
    both = jnp.concatenate([near, far], axis=1)
    table_orders = jnp.concatenate([both.reshape(-1), by_position[:, batch:].reshape(-1)])
    half_orders = both[0]
    full_orders = by_position[position, batch:]

    weights = lax.dynamic_slice_in_dim(lat_weight * math.sqrt(2.0 / lon_count), core * own_rows, own_rows)
    table = transposed_table(table_orders, lon_count)
    network = (w_in * 0.5, 0.5 * b_in[:, None], w_out, table)

    def send(x):
        shape = (positions, x.size // (positions * x.shape[-2] * x.shape[-1])) + x.shape[-2:]
        return lax.all_to_all(x.reshape(shape), everyone, split_axis=0, concat_axis=0, tiled=True)

    def cores_apart(arrays):
        count = arrays[0].shape[0] // 2
        return shift(jnp.concatenate([x[count:] for x in arrays], axis=0), 1)

    def transformed(chunk):
        start, rows = chunks[chunk]
        *by_link, rest = forward(
            half_levels,
            links,
            2 * pair,
            core_word,
            weights[start : start + rows],
            flat,
            lambda c: c * own_blocks + start // ROWS,
            others[chunk],
            *network,
        )
        return by_link, rest

    by_links, rests = [], []
    for chunk in range(len(chunks)):
        by_link, rest = transformed(chunk)
        if chunk == 0:
            rest, crossed, core, others[1] = lax.optimization_barrier((rest, crossed, core, others[1]))
            others += [swapped(cut_rows(*c, core)) for c in chunks[2:]]
        if chunk == 2:
            rests[1], rest = lax.optimization_barrier((rests[1], rest))
        by_links.append([shift(x, 2 * link) for link, x in enumerate(by_link)])
        rests.append(rest)
    full_pieces = [send(rests[0])]
    rests[1], full_pieces[0], by_links[:2] = lax.optimization_barrier(
        (rests[1], full_pieces[0], by_links[:2])
    )
    crossed, full_pieces[0] = lax.optimization_barrier((crossed, full_pieces[0]))
    crossed_too = lax.ppermute(crossed, "member", [(m, m ^ 1) for m in range(members)])
    full_pieces.append(send(rests[1]))
    rests[2], crossed_too, full_pieces[1], by_links[2:] = lax.optimization_barrier(
        (rests[2], crossed_too, full_pieces[1], by_links[2:])
    )
    full_pieces.append(send(rests[2]))
    half_pieces = []
    for by_link in by_links:
        apart = cores_apart(by_link)
        half_pieces.append(
            [(apart, (mask // 2) * pair) if mask % 2 else (by_link[mask // 2], 0) for mask in range(masks)]
        )

    near_legendre = lax.dynamic_slice(legendre, (0, 0, side * half_lats), (batch, degree_count, half_lats))
    far_legendre = [jnp.where(turn == 0, x, y) for x, y in ((crossed, crossed_too), (crossed_too, crossed))]
    half_legendre = jnp.concatenate([near_legendre, *far_legendre], axis=0)
    to_modal, to_levels = mode_matrices(modes, fields, half_levels)
    depth_lanes = jnp.tile(jnp.pad(depths, (0, LANES - levels)), 2)[None, :]
    matrices = (*to_modal, *to_levels, depth_lanes)
    half_step = functools.partial(spectral_half, place=place, orders=half_orders, pieces=half_pieces)
    near_values, far_values = [], []
    partials = [
        half_step(batch + part * share, share, legendre=half_legendre, got=None, matrices=None)
        for part in range(2)
    ]
    partials[0], matrices = lax.optimization_barrier((partials[0], matrices))
    first_sums = shift(partials[0], masks)
    partials[1], first_sums = lax.optimization_barrier((partials[1], first_sums))
    second_sums = shift(partials[1], masks)
    for part, sums in enumerate((first_sums, second_sums)):
        if part == 1:
            sums, near_values[0] = lax.optimization_barrier((sums, near_values[0]))
        values = half_step(part * share, share, legendre=half_legendre, got=sums, matrices=matrices)
        near_values.append(values)
        far_values.append(shift(values, masks))
    full_pieces[-1], near_values = lax.optimization_barrier((full_pieces[-1], near_values))
    last_rows = ROWS
    main, last = spectral_full(batch, last_rows, full_orders, full_pieces, legendre, matrices)
    main, far_values = lax.optimization_barrier((main, far_values))
    main = join(send(main))
    bands = synthesis_half(
        0, masks, place, half_orders, half_legendre, jnp.concatenate([*near_values, *far_values], axis=0)
    )
    bands = [shift(join(x), 2 * link) for link, x in enumerate(bands)]
    apart = cores_apart(bands)
    last, apart = lax.optimization_barrier((last, apart))
    last = join(send(last))
    near_bands = [(apart, mask // 2) if mask % 2 else (bands[mask // 2], 0) for mask in range(masks)]
    flat_table = table.reshape(-1, lon_count)
    main_rows = lat_rows - last_rows
    bands_at = lambda row: [(array, pair, block, row) for array, block in near_bands]
    full_slots = positions * (slots_dev - batch)
    bands = bands_at(0) + [(main, full_slots, 0, 0)]
    result = inverse(bands, main_rows, flat_table, lat_rows, 0, None)
    bands = bands_at(main_rows) + [(last, full_slots, 0, 0)]
    result = inverse(bands, last_rows, flat_table, lat_rows, main_rows, result)
    return result.reshape(grid.shape)


def body(grid, w_in, b_in, w_out, lat_weight, legendre, order_table, modes, depths):
    fields, half_levels, lat_rows, lon_count = grid.shape
    slots_dev = legendre.shape[0]
    count = 2 * fields * half_levels
    tiled = (
        lax.axis_size("lev") == 2
        and lat_rows % (2 * ROWS) == 0
        and lat_rows == 6 * ROWS
        and count == LANES + LANES // 2
        and half_levels * 2 <= LANES
        and half_levels % ROWS == 0
        and lon_count % 512 == 0
        and slots_dev % 16 == 0
        and lax.axis_size("lat") == 8
        and lax.axis_size("member") % 2 == 0
    )
    chosen = tiled_body if tiled else plain_body
    return chosen(grid, w_in, b_in, w_out, lat_weight, legendre, order_table, modes, depths)


def solution(mesh):
    in_specs = (
        P("member", "lev", "lat", None),
        P(),
        P(),
        P(),
        P("lat"),
        P(("lat", "lev"), None, None),
        P(),
        P(),
        P(),
    )
    out_specs = P("member", "lev", "lat", None)
    return jax.shard_map(body, mesh=mesh, in_specs=in_specs, out_specs=out_specs, check_vma=False)
```
